512 devices in a mesh: dp: 8 (over x, y_hi), ctx: 64 (over z, y_lo, core).
Axes of the slice: x: 4, y: 4 (y_hi: 2, y_lo: 2; y = y_hi * 2 + y_lo), z: 16, core: 2. Of those that a mesh axis runs over, the one named last changes fastest.
Arguments:
- query_proj: bfloat16 [8, 8192, 512], P('dp', 'ctx'), may hold values from -6 to 6
- key_proj: bfloat16 [8, 8192, 512], P('dp', 'ctx'), may hold values from -6 to 6
- value_proj: bfloat16 [8, 8192, 512], P('dp', 'ctx'), may hold values from -6 to 6
- long_filter: float32 [8192, 512], P(None, 'ctx'), may hold values from -2 to 2
- grad_output: bfloat16 [8, 8192, 512], P('dp', 'ctx'), may hold values from -6 to 6
Outputs:
- gated_output: bfloat16 [8, 8192, 512], P('dp', 'ctx')
- grad_query: bfloat16 [8, 8192, 512], P('dp', 'ctx')
- grad_key: bfloat16 [8, 8192, 512], P('dp', 'ctx')
- grad_value: bfloat16 [8, 8192, 512], P('dp', 'ctx')
- grad_filter: float32 [8192, 512], P(None, 'ctx')
The draws below stay inside these ranges and needn't reach their ends.
All inputs are finite; a program needn't handle non-finite values.
Results may differ from the reference program's by a relative error of at most 0.0057.
Values may be sent and summed in bfloat16 or wider, within the bound.
No kernel may reach another device: no remote copies, remote signals or barrier semaphores. Data moves between devices by JAX's collectives and lax.ppermute only.
A program may use at most 64 MiB of HBM per device.

```python
import math
import jax
import jax.numpy as jnp
from jax import lax

CHANNELS = 512
SEQS = 8
SEQ_LEN = 8192


def draw_long_filter(key, part):
    key = jax.random.fold_in(key, 11)
    pick_key, rate_key, noise_key = jax.random.split(key, 3)
    slow_share = 0.5
    slow = jax.random.uniform(pick_key, (CHANNELS,), jnp.float32) < slow_share
    unit = jax.random.uniform(rate_key, (CHANNELS,), jnp.float32)
    slow_rate = 0.2 / SEQ_LEN * jnp.exp(unit * math.log(10.0))
    fast_rate = 1.0 / 200.0 * jnp.exp(unit * math.log(200.0 / 30.0))
    rate = jnp.where(slow, slow_rate, fast_rate)
    scale = jnp.sqrt((1.0 - jnp.exp(-2.0 * rate)) / (1.0 - jnp.exp(-2.0 * rate * SEQ_LEN)))
    position = jnp.arange(SEQ_LEN, dtype=jnp.float32)
    noise = jnp.clip(jax.random.normal(noise_key, (SEQ_LEN, CHANNELS), jnp.float32), -5.0, 5.0)
    return noise * jnp.exp(-rate[None, :] * position[:, None]) * scale[None, :]


def level_of(rng, dims, cuts, least, top_value):
    level = 1.0
    for dim, shards_of in cuts:
        steps = jax.random.uniform(jax.random.fold_in(jax.random.fold_in(rng, 6), dim), (shards_of,), jnp.float32, least / len(cuts), top_value / len(cuts))
        level = level * jnp.repeat(jnp.exp(steps), dims[dim] // shards_of).reshape((-1,) + (1,) * (len(dims) - 1 - dim))
    return level


def gaussian(stream_key, shape, scale, reach, cuts=(), kind=jnp.bfloat16):
    array = scale * jax.random.normal(stream_key, shape, jnp.float32)
    if cuts:
        array = array * level_of(stream_key, shape, cuts, -0.22, 0.18)
    return jnp.clip(array, -reach, reach).astype(kind)


def setup_inputs(seed: int = 0) -> dict:
    streams_of = jax.random.split(jax.random.key(seed), 6)
    query_proj = gaussian(streams_of[0], (SEQS, SEQ_LEN, CHANNELS), 1.0, 6.0, ((0, 8), (1, 64)))
    key_proj = gaussian(streams_of[1], (SEQS, SEQ_LEN, CHANNELS), 1.0, 6.0, ((0, 8), (1, 64)))
    value_proj = gaussian(streams_of[2], (SEQS, SEQ_LEN, CHANNELS), 1.0, 6.0, ((0, 8), (1, 64)))
    long_filter = draw_long_filter(jax.random.fold_in(streams_of[5], 71), 0)
    grad_output = gaussian(streams_of[4], (SEQS, SEQ_LEN, CHANNELS), 1.0, 6.0, ((0, 8), (1, 64)))
    return {"query_proj": query_proj, "key_proj": key_proj, "value_proj": value_proj, "long_filter": long_filter, "grad_output": grad_output}


def reference(query_proj, key_proj, value_proj, long_filter, grad_output):
    mixed = (key_proj.astype(jnp.float32) * value_proj.astype(jnp.float32)).astype(jnp.bfloat16)
    grad_mix = (grad_output.astype(jnp.float32) * query_proj.astype(jnp.float32)).astype(jnp.bfloat16)
    length = 2 * SEQ_LEN
    filt_spec = jnp.fft.rfft(long_filter, n=length, axis=0)

    def one_sequence(pair):
        signal, cotangent = pair
        sig_spec = jnp.fft.rfft(signal.astype(jnp.float32), n=length, axis=0)
        cot_spec = jnp.fft.rfft(cotangent.astype(jnp.float32), n=length, axis=0)
        conv = jnp.fft.irfft(filt_spec * sig_spec, n=length, axis=0)[:SEQ_LEN]
        back = jnp.fft.irfft(jnp.conj(filt_spec) * cot_spec, n=length, axis=0)[:SEQ_LEN]
        taps = jnp.fft.irfft(jnp.conj(sig_spec) * cot_spec, n=length, axis=0)[:SEQ_LEN]
        return (conv.astype(jnp.bfloat16), back.astype(jnp.bfloat16), taps.astype(jnp.float32))
    conv, back, taps = lax.map(one_sequence, (mixed, grad_mix))
    gated_output = (query_proj.astype(jnp.float32) * conv.astype(jnp.float32)).astype(jnp.bfloat16)
    grad_query = (grad_output.astype(jnp.float32) * conv.astype(jnp.float32)).astype(jnp.bfloat16)
    grad_key = (back.astype(jnp.float32) * value_proj.astype(jnp.float32)).astype(jnp.bfloat16)
    grad_value = (back.astype(jnp.float32) * key_proj.astype(jnp.float32)).astype(jnp.bfloat16)
    grad_filter = lax.optimization_barrier(jnp.sum(taps, axis=0)) * (1.0 / math.sqrt(SEQ_LEN * SEQS))
    return (gated_output, grad_query, grad_key, grad_value, grad_filter)
```

```python
import math

import jax
import jax.numpy as jnp
from jax import lax
from jax.sharding import PartitionSpec as P

FACTOR = 128


HIGHEST = lax.Precision.HIGHEST


def dft_tables(length):
    index = jnp.arange(length, dtype=jnp.int32)
    product = index[:, None] * index[None, :] % length
    angle = 2.0 * math.pi / length * product.astype(jnp.float32)
    return (jnp.cos(angle), jnp.sin(angle))


def twiddle_tables(first, second):
    total = first * second
    rows = jnp.arange(first, dtype=jnp.int32)[:, None]
    cols = jnp.arange(second, dtype=jnp.int32)[None, :]
    angle = 2.0 * math.pi / total * (rows * cols % total).astype(jnp.float32)
    return (jnp.cos(angle), jnp.sin(angle))


def forward_transform(signal, tables):
    cos_one, sin_one, cos_two, sin_two, cos_turn, sin_turn = tables
    half = signal.shape[1]
    part_re = jnp.einsum("kn,cnm->ckm", cos_one[:, :half], signal, precision=HIGHEST)
    part_im = -jnp.einsum("kn,cnm->ckm", sin_one[:, :half], signal, precision=HIGHEST)
    turned_re = part_re * cos_turn + part_im * sin_turn
    turned_im = part_im * cos_turn - part_re * sin_turn
    spec_re = jnp.einsum("ckn,jn->ckj", turned_re, cos_two, precision=HIGHEST) + jnp.einsum(
        "ckn,jn->ckj", turned_im, sin_two, precision=HIGHEST
    )
    spec_im = jnp.einsum("ckn,jn->ckj", turned_im, cos_two, precision=HIGHEST) - jnp.einsum(
        "ckn,jn->ckj", turned_re, sin_two, precision=HIGHEST
    )
    return (spec_re, spec_im)


def inverse_transform(spec_re, spec_im, tables):
    cos_one, sin_one, cos_two, sin_two, cos_turn, sin_turn = tables
    first = cos_one.shape[0]
    second = cos_two.shape[0]
    half = first // 2
    back_re = jnp.einsum("ckj,nj->ckn", spec_re, cos_two, precision=HIGHEST) - jnp.einsum(
        "ckj,nj->ckn", spec_im, sin_two, precision=HIGHEST
    )
    back_im = jnp.einsum("ckj,nj->ckn", spec_im, cos_two, precision=HIGHEST) + jnp.einsum(
        "ckj,nj->ckn", spec_re, sin_two, precision=HIGHEST
    )
    turned_re = back_re * cos_turn - back_im * sin_turn
    turned_im = back_im * cos_turn + back_re * sin_turn
    signal = jnp.einsum("nk,ckm->cnm", cos_one[:half], turned_re, precision=HIGHEST) - jnp.einsum(
        "nk,ckm->cnm", sin_one[:half], turned_im, precision=HIGHEST
    )
    return signal * (1.0 / (first * second))


def on_device(query_proj, key_proj, value_proj, long_filter, grad_output):
    tok_count = query_proj.shape[1]
    width = query_proj.shape[2]
    groups = lax.axis_size("ctx")
    seqs = lax.axis_size("dp")
    seq_len = tok_count * groups
    share = width // groups
    first = FACTOR
    second = 2 * seq_len // first
    half = first // 2
    cos_one, sin_one = dft_tables(first)
    cos_two, sin_two = dft_tables(second)
    cos_turn, sin_turn = twiddle_tables(first, second)
    tables = (cos_one, sin_one, cos_two, sin_two, cos_turn, sin_turn)

    wide = jnp.float32
    mixed = (key_proj.astype(wide) * value_proj.astype(wide)).astype(jnp.bfloat16)[0]
    grad_mix = (grad_output.astype(wide) * query_proj.astype(wide)).astype(jnp.bfloat16)[0]
    both = jnp.stack([mixed.T.reshape(groups, share, tok_count), grad_mix.T.reshape(groups, share, tok_count)], axis=1)
    both = lax.all_to_all(both, "ctx", 0, 0)
    signal = both.transpose(1, 2, 0, 3).reshape(2 * share, half, second).astype(wide)

    filt_re, filt_im = forward_transform(long_filter.T.reshape(share, half, second), tables)
    spec_re, spec_im = forward_transform(signal, tables)
    mix_re, cot_re = spec_re[:share], spec_re[share:]
    mix_im, cot_im = spec_im[:share], spec_im[share:]
    factor = 1.0 / math.sqrt(seq_len * seqs)
    taps = inverse_transform(mix_re * cot_re + mix_im * cot_im, mix_re * cot_im - mix_im * cot_re, tables)
    taps = lax.all_to_all(taps.astype(jnp.bfloat16), "dp", 0, 0)

    prod_re = jnp.concatenate([filt_re * mix_re - filt_im * mix_im, filt_re * cot_re + filt_im * cot_im])
    prod_im = jnp.concatenate([filt_re * mix_im + filt_im * mix_re, filt_re * cot_im - filt_im * cot_re])
    out = inverse_transform(prod_re, prod_im, tables).astype(jnp.bfloat16)
    out = out.reshape(2, share, groups, tok_count).transpose(2, 0, 1, 3)
    out = lax.all_to_all(out, "ctx", 0, 0)

    summed = (jnp.sum(taps.astype(wide), axis=0) * factor).astype(jnp.bfloat16)
    grad_filter = lax.all_to_all(jnp.broadcast_to(summed[None], (seqs,) + summed.shape), "dp", 0, 0)
    grad_filter = grad_filter.astype(wide).reshape(share, seq_len).T

    conv_wide = out[:, 0].reshape(width, tok_count).T[None].astype(wide)
    back_wide = out[:, 1].reshape(width, tok_count).T[None].astype(wide)
    gated_output = (query_proj.astype(wide) * conv_wide).astype(jnp.bfloat16)
    grad_query = (grad_output.astype(wide) * conv_wide).astype(jnp.bfloat16)
    grad_key = (back_wide * value_proj.astype(wide)).astype(jnp.bfloat16)
    grad_value = (back_wide * key_proj.astype(wide)).astype(jnp.bfloat16)
    return (gated_output, grad_query, grad_key, grad_value, grad_filter)


def solution(mesh):
    in_specs = (
        P("dp", "ctx", None),
        P("dp", "ctx", None),
        P("dp", "ctx", None),
        P(None, "ctx"),
        P("dp", "ctx", None),
    )
    out_specs = (
        P("dp", "ctx", None),
        P("dp", "ctx", None),
        P("dp", "ctx", None),
        P("dp", "ctx", None),
        P(None, "ctx"),
    )
    return jax.shard_map(
        on_device, mesh=mesh, in_specs=in_specs, out_specs=out_specs, check_vma=False
    )
```

```python
import math

import jax
import jax.numpy as jnp
import ml_dtypes
import numpy as np
from jax import lax
from jax.experimental import pallas as pl
from jax.experimental.pallas import tpu as pltpu
from jax.sharding import PartitionSpec as P

BF = jnp.bfloat16
F32 = jnp.float32


def halves(table):
    high = table.astype(np.float32).astype(ml_dtypes.bfloat16)
    low = (table - high.astype(np.float64)).astype(np.float32).astype(ml_dtypes.bfloat16)
    return high, low


def make_tables(blocks, lanes):
    period = 2 * blocks
    total = period * lanes
    n = np.arange(blocks)
    odd = 2 * np.arange(blocks) + 1
    angle = math.pi / period * (n[None, :] * odd[:, None] % (2 * period))
    first = np.concatenate([np.cos(angle), -np.sin(angle)])
    m = np.arange(lanes)
    turn = math.pi / total * (odd[:, None] * m[None, :] % (2 * total))
    angle = 2 * math.pi / lanes * (m[:, None] * m[None, :] % lanes)
    cos, sin = np.cos(angle), np.sin(angle)
    second = np.block([[cos, -sin], [sin, cos]])
    a_high, a_low = halves(first)
    b_high, b_low = halves(first.T)
    g_high, g_low = halves(second)
    return dict(
        into=np.concatenate([a_high, a_low], axis=1),
        into3=np.concatenate([a_high, a_high, a_low], axis=1),
        out=np.block([[b_high, b_high], [b_low, np.zeros_like(b_low)]]),
        turn_cos=np.cos(turn).astype(np.float32),
        turn_sin=np.sin(turn).astype(np.float32),
        g_high=g_high,
        g_low=g_low,
    )


def dot(a, b):
    return jnp.dot(a, b, preferred_element_type=F32)


def split(x):
    high = x.astype(BF)
    return high, (x - high.astype(F32)).astype(BF)


def across(z_high, z_low, g_high, g_low):
    return dot(z_high, g_high) + dot(z_low, g_high) + dot(z_high, g_low)


def turned(part, blocks, cos, sin):
    re, im = part[:blocks], part[blocks:]
    return jnp.concatenate([re * cos + im * sin, im * cos - re * sin], axis=1)


def back_to_positions(spec, out_ref, cos, sin, blocks, lanes):
    count = spec.shape[0] // blocks
    result = []
    for pair in range(count // 2):
        rows = []
        for one in range(2):
            c = 2 * pair + one
            block = spec[c * blocks:(c + 1) * blocks]
            im, re = block[:, :lanes], block[:, lanes:]
            rows.append(jnp.concatenate([re * cos - im * sin, im * cos + re * sin], axis=0))
        both = jnp.concatenate(rows, axis=1)
        high, low = split(both)
        y = dot(out_ref[...], jnp.concatenate([high, low], axis=0))
        y = y[:blocks] + y[blocks:]
        result += [y[:, :lanes], y[:, lanes:]]
    return result


def filter_kernel(scale, f_ref, into3_ref, cos_ref, sin_ref, gh_ref, gl_ref, spec_ref):
    share, blocks, lanes = f_ref.shape
    cos, sin = cos_ref[...], sin_ref[...]
    rows = []
    for pair in range(share // 2):
        x = jnp.concatenate([f_ref[2 * pair], f_ref[2 * pair + 1]], axis=1)
        high, low = split(x)
        part = dot(into3_ref[...], jnp.concatenate([high, low, high], axis=0))
        rows.append(turned(part[:, :lanes], blocks, cos, sin))
        rows.append(turned(part[:, lanes:], blocks, cos, sin))
    high, low = split(jnp.concatenate(rows, axis=0))
    spec_ref[...] = across(high, low, gh_ref[...], gl_ref[...]) * scale


def conv_kernel(x_ref, filt_ref, into_ref, out_tab_ref, cos_ref, sin_ref, gh_ref, gl_ref, y_ref, spec_ref, wide_ref):
    blocks, fields, lanes = x_ref.shape
    share = fields // 2
    cos, sin = cos_ref[...], sin_ref[...]
    wide_ref[...] = x_ref[...].astype(F32).reshape(blocks * fields, lanes)
    rows = []
    for pair in range(fields // 2):
        x = jnp.concatenate(
            [wide_ref[pl.ds(2 * pair + one, blocks, stride=fields), :] for one in range(2)], axis=1
        ).astype(BF)
        part = dot(into_ref[...], jnp.concatenate([x, x], axis=0))
        rows.append(turned(part[:, :lanes], blocks, cos, sin))
        rows.append(turned(part[:, lanes:], blocks, cos, sin))
    high, low = split(jnp.concatenate(rows, axis=0))
    spec_ref[...] = across(high, low, gh_ref[...], gl_ref[...])
    half = share * blocks
    fr, fi = filt_ref[:, :lanes], filt_ref[:, lanes:]
    xr, xi = spec_ref[:half, :lanes], spec_ref[:half, lanes:]
    gr, gi = spec_ref[half:, :lanes], spec_ref[half:, lanes:]
    conv = jnp.concatenate([fr * xi + fi * xr, fr * xr - fi * xi], axis=1)
    back = jnp.concatenate([fr * gi - fi * gr, fr * gr + fi * gi], axis=1)
    high, low = split(jnp.concatenate([conv, back], axis=0))
    inner = across(high, low, gh_ref[...], gl_ref[...])
    ys = back_to_positions(inner, out_tab_ref, cos, sin, blocks, lanes)
    for f, y in enumerate(ys):
        wide_ref[pl.ds(f, blocks, stride=fields), :] = y
    y_ref[...] = wide_ref[...].reshape(blocks, fields, lanes).astype(BF)


def taps_kernel(scale, spec_ref, out_tab_ref, cos_ref, sin_ref, gh_ref, gl_ref, taps_ref, wide_ref):
    blocks, lanes = cos_ref.shape
    half = spec_ref.shape[0] // 2
    share = half // blocks
    cos, sin = cos_ref[...], sin_ref[...]
    xr, xi = spec_ref[:half, :lanes], spec_ref[:half, lanes:]
    gr, gi = spec_ref[half:, :lanes], spec_ref[half:, lanes:]
    prod = jnp.concatenate([xr * gi - xi * gr, xr * gr + xi * gi], axis=1)
    high, low = split(prod * scale)
    inner = across(high, low, gh_ref[...], gl_ref[...])
    for c, y in enumerate(back_to_positions(inner, out_tab_ref, cos, sin, blocks, lanes)):
        wide_ref[pl.ds(c, blocks, stride=share), :] = y
    taps_ref[...] = wide_ref[...].astype(BF)


def mix_kernel(q_ref, k_ref, v_ref, g_ref, out_ref):
    groups, fields, lanes = out_ref.shape
    share = fields // 2

    def turn(a, b):
        prod = (a[0].astype(F32) * b[0].astype(F32)).astype(BF).astype(F32)
        return prod.T.reshape(groups, share, lanes)

    both = jnp.concatenate([turn(k_ref, v_ref), turn(g_ref, q_ref)], axis=1)
    out_ref[...] = both.astype(BF)


def gate_kernel(y_ref, q_ref, k_ref, v_ref, g_ref, go_ref, gq_ref, gk_ref, gv_ref):
    groups, fields, lanes = y_ref.shape
    share = fields // 2
    both = y_ref[...].astype(F32)
    conv = both[:, :share].reshape(groups * share, lanes).T
    back = both[:, share:].reshape(groups * share, lanes).T
    go_ref[0] = (q_ref[0].astype(F32) * conv).astype(BF)
    gq_ref[0] = (g_ref[0].astype(F32) * conv).astype(BF)
    gk_ref[0] = (back * v_ref[0].astype(F32)).astype(BF)
    gv_ref[0] = (back * k_ref[0].astype(F32)).astype(BF)


PARAMS = pltpu.CompilerParams(vmem_limit_bytes=32 * 1024 * 1024)


def on_device(query_proj, key_proj, value_proj, long_filter, grad_output):
    tok_count = query_proj.shape[1]
    width = query_proj.shape[2]
    groups = lax.axis_size("ctx")
    seqs = lax.axis_size("dp")
    seq_len = tok_count * groups
    share = width // groups
    t = make_tables(groups, tok_count)
    spec_rows = share * groups

    both = pl.pallas_call(
        mix_kernel,
        out_shape=jax.ShapeDtypeStruct((groups, 2 * share, tok_count), BF),
        compiler_params=PARAMS,
    )(query_proj, key_proj, value_proj, grad_output)
    both = lax.all_to_all(both, "ctx", 0, 0)

    filt_spec = pl.pallas_call(
        lambda *refs: filter_kernel(2.0 / (2 * seq_len), *refs),
        out_shape=jax.ShapeDtypeStruct((spec_rows, 2 * tok_count), F32),
        compiler_params=PARAMS,
    )(long_filter.T.reshape(share, groups, tok_count), t["into3"], t["turn_cos"], t["turn_sin"], t["g_high"], t["g_low"])

    out, spec = pl.pallas_call(
        conv_kernel,
        out_shape=(
            jax.ShapeDtypeStruct((groups, 2 * share, tok_count), BF),
            jax.ShapeDtypeStruct((2 * spec_rows, 2 * tok_count), F32),
        ),
        scratch_shapes=[pltpu.VMEM((2 * spec_rows, tok_count), F32)],
        compiler_params=PARAMS,
    )(both, filt_spec, t["into"], t["out"], t["turn_cos"], t["turn_sin"], t["g_high"], t["g_low"])
    out = lax.all_to_all(out, "ctx", 0, 0)

    factor = 1.0 / math.sqrt(seq_len * seqs)
    taps = pl.pallas_call(
        lambda *refs: taps_kernel(factor * 2.0 / (2 * seq_len), *refs),
        out_shape=jax.ShapeDtypeStruct((spec_rows, tok_count), BF),
        scratch_shapes=[pltpu.VMEM((spec_rows, tok_count), F32)],
        compiler_params=PARAMS,
    )(spec, t["out"], t["turn_cos"], t["turn_sin"], t["g_high"], t["g_low"])
    for flip in (1, 2, 6):
        taps = taps.astype(BF)
        other = lax.ppermute(taps, "dp", [(i, i ^ flip) for i in range(seqs)])
        taps = taps.astype(F32) + other.astype(F32)
    grad_filter = taps.reshape(groups, share, tok_count).transpose(0, 2, 1).reshape(seq_len, share)

    grads = pl.pallas_call(
        gate_kernel,
        out_shape=[jax.ShapeDtypeStruct(query_proj.shape, BF)] * 4,
        compiler_params=PARAMS,
    )(out, query_proj, key_proj, value_proj, grad_output)
    return (*grads, grad_filter)


def solution(mesh):
    tokens = P("dp", "ctx", None)
    taps = P(None, "ctx")
    return jax.shard_map(
        on_device,
        mesh=mesh,
        in_specs=(tokens, tokens, tokens, taps, tokens),
        out_specs=(tokens, tokens, tokens, tokens, taps),
        check_vma=False,
    )
```

```python
import math

import jax
import jax.numpy as jnp
import ml_dtypes
import numpy as np
from jax import lax
from jax.experimental import pallas as pl
from jax.experimental.pallas import tpu as pltpu
from jax.sharding import PartitionSpec as P

BF = jnp.bfloat16
F32 = jnp.float32


def halves(table):
    high = table.astype(np.float32).astype(ml_dtypes.bfloat16)
    low = (table - high.astype(np.float64)).astype(np.float32).astype(ml_dtypes.bfloat16)
    return high, low


def make_tables(blocks, lanes):
    period = 2 * blocks
    total = period * lanes
    n = np.arange(blocks)
    odd = 2 * np.arange(blocks) + 1
    angle = math.pi / period * (n[None, :] * odd[:, None] % (2 * period))
    first = np.concatenate([np.cos(angle), -np.sin(angle)])
    m = np.arange(lanes)
    turn = math.pi / total * (odd[:, None] * m[None, :] % (2 * total))
    angle = 2 * math.pi / lanes * (m[:, None] * m[None, :] % lanes)
    cos, sin = np.cos(angle), np.sin(angle)
    second = np.block([[cos, -sin], [sin, cos]])
    a_high, a_low = halves(first)
    b_high, b_low = halves(first.T)
    g_high, g_low = halves(second)
    return dict(
        into=np.concatenate([a_high, a_low], axis=1),
        into3=np.concatenate([a_high, a_high, a_low], axis=1),
        out=np.block([[b_high, b_high], [b_low, np.zeros_like(b_low)]]),
        turn_cos=np.cos(turn).astype(np.float32),
        turn_sin=np.sin(turn).astype(np.float32),
        g_high=g_high,
        g_low=g_low,
    )


def dot(a, b):
    return jnp.dot(a, b, preferred_element_type=F32)


def split(x):
    high = x.astype(BF)
    return high, (x - high.astype(F32)).astype(BF)


def across(z_high, z_low, g_high, g_low):
    return dot(z_high, g_high) + dot(z_low, g_high) + dot(z_high, g_low)


def turned(part, blocks, cos, sin):
    re, im = part[:blocks], part[blocks:]
    return jnp.concatenate([re * cos + im * sin, im * cos - re * sin], axis=1)


def back_to_positions(spec, out_ref, cos, sin, blocks, lanes):
    count = spec.shape[0] // blocks
    result = []
    for pair in range(count // 2):
        rows = []
        for one in range(2):
            c = 2 * pair + one
            block = spec[c * blocks:(c + 1) * blocks]
            im, re = block[:, :lanes], block[:, lanes:]
            rows.append(jnp.concatenate([re * cos - im * sin, im * cos + re * sin], axis=0))
        both = jnp.concatenate(rows, axis=1)
        high, low = split(both)
        y = dot(out_ref[...], jnp.concatenate([high, low], axis=0))
        y = y[:blocks] + y[blocks:]
        result += [y[:, :lanes], y[:, lanes:]]
    return result


def filter_kernel(scale, f_ref, into3_ref, cos_ref, sin_ref, gh_ref, gl_ref, spec_ref):
    share, blocks, lanes = f_ref.shape
    cos, sin = cos_ref[...], sin_ref[...]
    rows = []
    for pair in range(share // 2):
        x = jnp.concatenate([f_ref[2 * pair], f_ref[2 * pair + 1]], axis=1)
        high, low = split(x)
        part = dot(into3_ref[...], jnp.concatenate([high, low, high], axis=0))
        rows.append(turned(part[:, :lanes], blocks, cos, sin))
        rows.append(turned(part[:, lanes:], blocks, cos, sin))
    high, low = split(jnp.concatenate(rows, axis=0))
    spec_ref[...] = across(high, low, gh_ref[...], gl_ref[...]) * scale


def conv_kernel(x_ref, filt_ref, into_ref, out_tab_ref, cos_ref, sin_ref, gh_ref, gl_ref, y_ref, spec_ref, wide_ref):
    blocks, fields, lanes = x_ref.shape
    share = fields // 2
    cos, sin = cos_ref[...], sin_ref[...]
    wide_ref[...] = x_ref[...].astype(F32).reshape(blocks * fields, lanes)
    rows = []
    for pair in range(fields // 2):
        x = jnp.concatenate(
            [wide_ref[pl.ds(2 * pair + one, blocks, stride=fields), :] for one in range(2)], axis=1
        ).astype(BF)
        part = dot(into_ref[...], jnp.concatenate([x, x], axis=0))
        rows.append(turned(part[:, :lanes], blocks, cos, sin))
        rows.append(turned(part[:, lanes:], blocks, cos, sin))
    high, low = split(jnp.concatenate(rows, axis=0))
    spec_ref[...] = across(high, low, gh_ref[...], gl_ref[...])
    half = share * blocks
    fr, fi = filt_ref[:, :lanes], filt_ref[:, lanes:]
    xr, xi = spec_ref[:half, :lanes], spec_ref[:half, lanes:]
    gr, gi = spec_ref[half:, :lanes], spec_ref[half:, lanes:]
    conv = jnp.concatenate([fr * xi + fi * xr, fr * xr - fi * xi], axis=1)
    back = jnp.concatenate([fr * gi - fi * gr, fr * gr + fi * gi], axis=1)
    high, low = split(jnp.concatenate([conv, back], axis=0))
    inner = across(high, low, gh_ref[...], gl_ref[...])
    ys = back_to_positions(inner, out_tab_ref, cos, sin, blocks, lanes)
    for f, y in enumerate(ys):
        wide_ref[pl.ds(f, blocks, stride=fields), :] = y
    y_ref[...] = wide_ref[...].reshape(blocks, fields, lanes).astype(BF)


def taps_kernel(scale, spec_ref, out_tab_ref, cos_ref, sin_ref, gh_ref, gl_ref, taps_ref, wide_ref):
    blocks, lanes = cos_ref.shape
    half = spec_ref.shape[0] // 2
    share = half // blocks
    cos, sin = cos_ref[...], sin_ref[...]
    xr, xi = spec_ref[:half, :lanes], spec_ref[:half, lanes:]
    gr, gi = spec_ref[half:, :lanes], spec_ref[half:, lanes:]
    prod = jnp.concatenate([xr * gi - xi * gr, xr * gr + xi * gi], axis=1)
    high, low = split(prod * scale)
    inner = across(high, low, gh_ref[...], gl_ref[...])
    for c, y in enumerate(back_to_positions(inner, out_tab_ref, cos, sin, blocks, lanes)):
        wide_ref[pl.ds(c, blocks, stride=share), :] = y
    taps_ref[...] = wide_ref[...].astype(BF)


def mix_kernel(q_hbm, k_hbm, v_hbm, g_hbm, out_ref, q_ref, k_ref, v_ref, g_ref, sems):
    groups, fields, lanes = out_ref.shape
    share = fields // 2
    copies = [
        pltpu.make_async_copy(source, target, sems.at[i])
        for i, (source, target) in enumerate(
            [(k_hbm, k_ref), (v_hbm, v_ref), (g_hbm, g_ref), (q_hbm, q_ref)]
        )
    ]
    for copy in copies:
        copy.start()

    def turn(a, b):
        prod = (a[0].astype(F32) * b[0].astype(F32)).astype(BF).astype(F32)
        return prod.T.reshape(groups, share, lanes)

    copies[0].wait()
    copies[1].wait()
    mixed = turn(k_ref, v_ref)
    copies[2].wait()
    copies[3].wait()
    out_ref[...] = jnp.concatenate([mixed, turn(g_ref, q_ref)], axis=1).astype(BF)


def gate_kernel(y_ref, q_ref, k_ref, v_ref, g_ref, go_ref, gq_ref, gk_ref, gv_ref):
    groups, fields, lanes = y_ref.shape
    share = fields // 2
    both = y_ref[...].astype(F32)
    conv = both[:, :share].reshape(groups * share, lanes).T
    back = both[:, share:].reshape(groups * share, lanes).T
    go_ref[0] = (q_ref[0].astype(F32) * conv).astype(BF)
    gq_ref[0] = (g_ref[0].astype(F32) * conv).astype(BF)
    gk_ref[0] = (back * v_ref[0].astype(F32)).astype(BF)
    gv_ref[0] = (back * k_ref[0].astype(F32)).astype(BF)


PARAMS = pltpu.CompilerParams(vmem_limit_bytes=32 * 1024 * 1024)


def on_device(query_proj, key_proj, value_proj, long_filter, grad_output):
    tok_count = query_proj.shape[1]
    width = query_proj.shape[2]
    groups = lax.axis_size("ctx")
    seqs = lax.axis_size("dp")
    seq_len = tok_count * groups
    share = width // groups
    t = make_tables(groups, tok_count)
    spec_rows = share * groups

    both = pl.pallas_call(
        mix_kernel,
        out_shape=jax.ShapeDtypeStruct((groups, 2 * share, tok_count), BF),
        in_specs=[pl.BlockSpec(memory_space=pltpu.HBM)] * 4,
        scratch_shapes=[pltpu.VMEM(query_proj.shape, BF)] * 4 + [pltpu.SemaphoreType.DMA((4,))],
        compiler_params=pltpu.CompilerParams(vmem_limit_bytes=60 * 1024 * 1024),
    )(query_proj, key_proj, value_proj, grad_output)
    both = lax.all_to_all(both, "ctx", 0, 0)

    filt_spec = pl.pallas_call(
        lambda *refs: filter_kernel(2.0 / (2 * seq_len), *refs),
        out_shape=jax.ShapeDtypeStruct((spec_rows, 2 * tok_count), F32),
        compiler_params=PARAMS,
    )(long_filter.T.reshape(share, groups, tok_count), t["into3"], t["turn_cos"], t["turn_sin"], t["g_high"], t["g_low"])

    out, spec = pl.pallas_call(
        conv_kernel,
        out_shape=(
            jax.ShapeDtypeStruct((groups, 2 * share, tok_count), BF),
            jax.ShapeDtypeStruct((2 * spec_rows, 2 * tok_count), F32),
        ),
        scratch_shapes=[pltpu.VMEM((2 * spec_rows, tok_count), F32)],
        compiler_params=PARAMS,
    )(both, filt_spec, t["into"], t["out"], t["turn_cos"], t["turn_sin"], t["g_high"], t["g_low"])
    out = lax.all_to_all(out, "ctx", 0, 0)

    factor = 1.0 / math.sqrt(seq_len * seqs)
    taps = pl.pallas_call(
        lambda *refs: taps_kernel(factor * 2.0 / (2 * seq_len), *refs),
        out_shape=jax.ShapeDtypeStruct((spec_rows, tok_count), BF),
        scratch_shapes=[pltpu.VMEM((spec_rows, tok_count), F32)],
        compiler_params=PARAMS,
    )(spec, t["out"], t["turn_cos"], t["turn_sin"], t["g_high"], t["g_low"])
    def exchanged(part):
        for flip in (1, 2, 6):
            part = part.astype(BF)
            other = lax.ppermute(part, "dp", [(i, i ^ flip) for i in range(seqs)])
            part = part.astype(F32) + other.astype(F32)
        return part

    cut = spec_rows * 3 // 8
    taps = jnp.concatenate([exchanged(taps[:cut]), exchanged(taps[cut:])])
    grad_filter = taps.reshape(groups, share, tok_count).transpose(0, 2, 1).reshape(seq_len, share)

    grads = pl.pallas_call(
        gate_kernel,
        out_shape=[jax.ShapeDtypeStruct(query_proj.shape, BF)] * 4,
        compiler_params=PARAMS,
    )(out, query_proj, key_proj, value_proj, grad_output)
    return (*grads, grad_filter)


def solution(mesh):
    tokens = P("dp", "ctx", None)
    taps = P(None, "ctx")
    return jax.shard_map(
        on_device,
        mesh=mesh,
        in_specs=(tokens, tokens, tokens, taps, tokens),
        out_specs=(tokens, tokens, tokens, tokens, taps),
        check_vma=False,
    )
```

```python
import math

import jax
import jax.numpy as jnp
import ml_dtypes
import numpy as np
from jax import lax
from jax.experimental import pallas as pl
from jax.experimental.pallas import tpu as pltpu
from jax.sharding import PartitionSpec as P

BF = jnp.bfloat16
F32 = jnp.float32


def halves(table):
    high = table.astype(np.float32).astype(ml_dtypes.bfloat16)
    low = (table - high.astype(np.float64)).astype(np.float32).astype(ml_dtypes.bfloat16)
    return high, low


def make_tables(blocks, lanes):
    period = 2 * blocks
    total = period * lanes
    n = np.arange(blocks)
    odd = 2 * np.arange(blocks) + 1
    angle = math.pi / period * (n[None, :] * odd[:, None] % (2 * period))
    first = np.concatenate([np.cos(angle), -np.sin(angle)])
    m = np.arange(lanes)
    turn = math.pi / total * (odd[:, None] * m[None, :] % (2 * total))
    angle = 2 * math.pi / lanes * (m[:, None] * m[None, :] % lanes)
    cos, sin = np.cos(angle), np.sin(angle)
    second = np.block([[cos, -sin], [sin, cos]])
    a_high, a_low = halves(first)
    b_high, b_low = halves(first.T)
    g_high, g_low = halves(second)
    return dict(
        into=np.concatenate([a_high, a_low], axis=1),
        into3=np.concatenate([a_high, a_high, a_low], axis=1),
        out=np.block([[b_high, b_high], [b_low, np.zeros_like(b_low)]]),
        turn_cos=np.cos(turn).astype(np.float32),
        turn_sin=np.sin(turn).astype(np.float32),
        g_high=g_high,
        g_low=g_low,
    )


def dot(a, b):
    return jnp.dot(a, b, preferred_element_type=F32)


def split(x):
    high = x.astype(BF)
    return high, (x - high.astype(F32)).astype(BF)


def across(z_high, z_low, g_high, g_low):
    return dot(z_high, g_high) + dot(z_low, g_high) + dot(z_high, g_low)


def turned(part, blocks, cos, sin):
    re, im = part[:blocks], part[blocks:]
    return jnp.concatenate([re * cos + im * sin, im * cos - re * sin], axis=1)


def back_to_positions(spec, out_ref, cos, sin, blocks, lanes):
    count = spec.shape[0] // blocks
    result = []
    for pair in range(count // 2):
        rows = []
        for one in range(2):
            c = 2 * pair + one
            block = spec[c * blocks:(c + 1) * blocks]
            im, re = block[:, :lanes], block[:, lanes:]
            rows.append(jnp.concatenate([re * cos - im * sin, im * cos + re * sin], axis=0))
        both = jnp.concatenate(rows, axis=1)
        high, low = split(both)
        y = dot(out_ref[...], jnp.concatenate([high, low], axis=0))
        y = y[:blocks] + y[blocks:]
        result += [y[:, :lanes], y[:, lanes:]]
    return result


def filter_kernel(scale, f_ref, into3_ref, cos_ref, sin_ref, gh_ref, gl_ref, spec_ref):
    share, blocks, lanes = f_ref.shape
    cos, sin = cos_ref[...], sin_ref[...]
    rows = []
    for pair in range(share // 2):
        x = jnp.concatenate([f_ref[2 * pair], f_ref[2 * pair + 1]], axis=1)
        high, low = split(x)
        part = dot(into3_ref[...], jnp.concatenate([high, low, high], axis=0))
        rows.append(turned(part[:, :lanes], blocks, cos, sin))
        rows.append(turned(part[:, lanes:], blocks, cos, sin))
    high, low = split(jnp.concatenate(rows, axis=0))
    spec_ref[...] = across(high, low, gh_ref[...], gl_ref[...]) * scale


def conv_kernel(x_ref, filt_ref, into_ref, out_tab_ref, cos_ref, sin_ref, gh_ref, gl_ref, y_ref, spec_ref, wide_ref):
    blocks, fields, lanes = x_ref.shape
    share = fields // 2
    cos, sin = cos_ref[...], sin_ref[...]
    wide_ref[...] = x_ref[...].astype(F32).reshape(blocks * fields, lanes)
    rows = []
    for pair in range(fields // 2):
        x = jnp.concatenate(
            [wide_ref[pl.ds(2 * pair + one, blocks, stride=fields), :] for one in range(2)], axis=1
        ).astype(BF)
        part = dot(into_ref[...], jnp.concatenate([x, x], axis=0))
        rows.append(turned(part[:, :lanes], blocks, cos, sin))
        rows.append(turned(part[:, lanes:], blocks, cos, sin))
    high, low = split(jnp.concatenate(rows, axis=0))
    spec_ref[...] = across(high, low, gh_ref[...], gl_ref[...])
    half = share * blocks
    fr, fi = filt_ref[:, :lanes], filt_ref[:, lanes:]
    xr, xi = spec_ref[:half, :lanes], spec_ref[:half, lanes:]
    gr, gi = spec_ref[half:, :lanes], spec_ref[half:, lanes:]
    conv = jnp.concatenate([fr * xi + fi * xr, fr * xr - fi * xi], axis=1)
    back = jnp.concatenate([fr * gi - fi * gr, fr * gr + fi * gi], axis=1)
    high, low = split(jnp.concatenate([conv, back], axis=0))
    inner = across(high, low, gh_ref[...], gl_ref[...])
    ys = back_to_positions(inner, out_tab_ref, cos, sin, blocks, lanes)
    for f, y in enumerate(ys):
        wide_ref[pl.ds(f, blocks, stride=fields), :] = y
    y_ref[...] = wide_ref[...].reshape(blocks, fields, lanes).astype(BF)


def taps_kernel(scale, spec_ref, out_tab_ref, cos_ref, sin_ref, gh_ref, gl_ref, taps_ref, wide_ref):
    blocks, lanes = cos_ref.shape
    half = spec_ref.shape[0] // 2
    share = half // blocks
    cos, sin = cos_ref[...], sin_ref[...]
    xr, xi = spec_ref[:half, :lanes], spec_ref[:half, lanes:]
    gr, gi = spec_ref[half:, :lanes], spec_ref[half:, lanes:]
    prod = jnp.concatenate([xr * gi - xi * gr, xr * gr + xi * gi], axis=1)
    high, low = split(prod * scale)
    inner = across(high, low, gh_ref[...], gl_ref[...])
    for c, y in enumerate(back_to_positions(inner, out_tab_ref, cos, sin, blocks, lanes)):
        wide_ref[pl.ds(c, blocks, stride=share), :] = y
    taps_ref[...] = wide_ref[...].astype(BF)


def mix_kernel(q_hbm, k_hbm, v_hbm, g_hbm, out_ref, q_ref, k_ref, v_ref, g_ref, sems):
    groups, fields, lanes = out_ref.shape
    share = fields // 2
    copies = [
        pltpu.make_async_copy(source, target, sems.at[i])
        for i, (source, target) in enumerate(
            [(k_hbm, k_ref), (v_hbm, v_ref), (g_hbm, g_ref), (q_hbm, q_ref)]
        )
    ]
    for copy in copies:
        copy.start()

    def turn(a, b):
        prod = (a[0].astype(F32) * b[0].astype(F32)).astype(BF).astype(F32)
        return prod.T.reshape(groups, share, lanes)

    copies[0].wait()
    copies[1].wait()
    mixed = turn(k_ref, v_ref)
    copies[2].wait()
    copies[3].wait()
    out_ref[...] = jnp.concatenate([mixed, turn(g_ref, q_ref)], axis=1).astype(BF)


def gate_kernel(y_ref, mine_ref, other_ref, q_ref, k_ref, v_ref, g_ref, go_ref, gq_ref, gk_ref, gv_ref, taps_ref):
    taps_ref[...] = mine_ref[...].astype(F32) + other_ref[...].astype(F32)
    groups, fields, lanes = y_ref.shape
    share = fields // 2
    both = y_ref[...].astype(F32)
    conv = both[:, :share].reshape(groups * share, lanes).T
    back = both[:, share:].reshape(groups * share, lanes).T
    go_ref[0] = (q_ref[0].astype(F32) * conv).astype(BF)
    gq_ref[0] = (g_ref[0].astype(F32) * conv).astype(BF)
    gk_ref[0] = (back * v_ref[0].astype(F32)).astype(BF)
    gv_ref[0] = (back * k_ref[0].astype(F32)).astype(BF)


PARAMS = pltpu.CompilerParams(vmem_limit_bytes=32 * 1024 * 1024)


def on_device(query_proj, key_proj, value_proj, long_filter, grad_output):
    tok_count = query_proj.shape[1]
    width = query_proj.shape[2]
    groups = lax.axis_size("ctx")
    seqs = lax.axis_size("dp")
    seq_len = tok_count * groups
    share = width // groups
    t = make_tables(groups, tok_count)
    spec_rows = share * groups

    both = pl.pallas_call(
        mix_kernel,
        out_shape=jax.ShapeDtypeStruct((groups, 2 * share, tok_count), BF),
        in_specs=[pl.BlockSpec(memory_space=pltpu.HBM)] * 4,
        scratch_shapes=[pltpu.VMEM(query_proj.shape, BF)] * 4 + [pltpu.SemaphoreType.DMA((4,))],
        compiler_params=pltpu.CompilerParams(vmem_limit_bytes=60 * 1024 * 1024),
    )(query_proj, key_proj, value_proj, grad_output)
    both = lax.all_to_all(both, "ctx", 0, 0)

    filt_spec = pl.pallas_call(
        lambda *refs: filter_kernel(2.0 / (2 * seq_len), *refs),
        out_shape=jax.ShapeDtypeStruct((spec_rows, 2 * tok_count), F32),
        compiler_params=PARAMS,
    )(long_filter.T.reshape(share, groups, tok_count), t["into3"], t["turn_cos"], t["turn_sin"], t["g_high"], t["g_low"])

    out, spec = pl.pallas_call(
        conv_kernel,
        out_shape=(
            jax.ShapeDtypeStruct((groups, 2 * share, tok_count), BF),
            jax.ShapeDtypeStruct((2 * spec_rows, 2 * tok_count), F32),
        ),
        scratch_shapes=[pltpu.VMEM((2 * spec_rows, tok_count), F32)],
        compiler_params=PARAMS,
    )(both, filt_spec, t["into"], t["out"], t["turn_cos"], t["turn_sin"], t["g_high"], t["g_low"])
    out = lax.all_to_all(out, "ctx", 0, 0)

    factor = 1.0 / math.sqrt(seq_len * seqs)
    taps = pl.pallas_call(
        lambda *refs: taps_kernel(factor * 2.0 / (2 * seq_len), *refs),
        out_shape=jax.ShapeDtypeStruct((spec_rows, tok_count), BF),
        scratch_shapes=[pltpu.VMEM((spec_rows, tok_count), F32)],
        compiler_params=PARAMS,
    )(spec, t["out"], t["turn_cos"], t["turn_sin"], t["g_high"], t["g_low"])
    def swap(part, flip):
        return lax.ppermute(part, "dp", [(i, i ^ flip) for i in range(seqs)])

    def add(a, b):
        return (a.astype(F32) + b.astype(F32)).astype(BF)

    for flip in (1, 2):
        taps = add(taps, swap(taps, flip))
    other = swap(taps, 6)

    *grads, grad_filter = pl.pallas_call(
        gate_kernel,
        out_shape=[jax.ShapeDtypeStruct(query_proj.shape, BF)] * 4 + [jax.ShapeDtypeStruct(taps.shape, F32)],
        compiler_params=PARAMS,
    )(out, taps, other, query_proj, key_proj, value_proj, grad_output)
    grad_filter = grad_filter.reshape(groups, share, tok_count).transpose(0, 2, 1).reshape(seq_len, share)
    return (*grads, grad_filter)


def solution(mesh):
    tokens = P("dp", "ctx", None)
    taps = P(None, "ctx")
    return jax.shard_map(
        on_device,
        mesh=mesh,
        in_specs=(tokens, tokens, tokens, taps, tokens),
        out_specs=(tokens, tokens, tokens, tokens, taps),
        check_vma=False,
    )
```

```python
import math

import jax
import jax.numpy as jnp
import ml_dtypes
import numpy as np
from jax import lax
from jax.experimental import pallas as pl
from jax.experimental.pallas import tpu as pltpu
from jax.sharding import PartitionSpec as P

BF = jnp.bfloat16
F32 = jnp.float32


def halves(table):
    high = table.astype(np.float32).astype(ml_dtypes.bfloat16)
    low = (table - high.astype(np.float64)).astype(np.float32).astype(ml_dtypes.bfloat16)
    return high, low


def make_tables(blocks, lanes):
    period = 2 * blocks
    total = period * lanes
    n = np.arange(blocks)
    odd = 2 * np.arange(blocks) + 1
    angle = math.pi / period * (n[None, :] * odd[:, None] % (2 * period))
    first = np.concatenate([np.cos(angle), -np.sin(angle)])
    m = np.arange(lanes)
    turn = math.pi / total * (odd[:, None] * m[None, :] % (2 * total))
    angle = 2 * math.pi / lanes * (m[:, None] * m[None, :] % lanes)
    cos, sin = np.cos(angle), np.sin(angle)
    second = np.block([[cos, -sin], [sin, cos]])
    a_high, a_low = halves(first)
    b_high, b_low = halves(first.T)
    g_high, g_low = halves(second)
    return dict(
        into=np.concatenate([a_high, a_low], axis=1),
        into3=np.concatenate([a_high, a_high, a_low], axis=1),
        out=np.block([[b_high, b_high], [b_low, np.zeros_like(b_low)]]),
        turn_cos=np.cos(turn).astype(np.float32),
        turn_sin=np.sin(turn).astype(np.float32),
        g_high=g_high,
        g_low=g_low,
    )


def dot(a, b):
    return jnp.dot(a, b, preferred_element_type=F32)


def split(x):
    high = x.astype(BF)
    return high, (x - high.astype(F32)).astype(BF)


def across(z_high, z_low, g_high, g_low):
    return dot(z_high, g_high) + dot(z_low, g_high) + dot(z_high, g_low)


def turned(part, blocks, cos, sin):
    re, im = part[:blocks], part[blocks:]
    return jnp.concatenate([re * cos + im * sin, im * cos - re * sin], axis=1)


def back_to_positions(spec, out_ref, cos, sin, blocks, lanes):
    count = spec.shape[0] // blocks
    result = []
    for pair in range(count // 2):
        rows = []
        for one in range(2):
            c = 2 * pair + one
            block = spec[c * blocks:(c + 1) * blocks]
            im, re = block[:, :lanes], block[:, lanes:]
            rows.append(jnp.concatenate([re * cos - im * sin, im * cos + re * sin], axis=0))
        both = jnp.concatenate(rows, axis=1)
        high, low = split(both)
        y = dot(out_ref[...], jnp.concatenate([high, low], axis=0))
        y = y[:blocks] + y[blocks:]
        result += [y[:, :lanes], y[:, lanes:]]
    return result


def filter_kernel(scale, f_ref, into3_ref, cos_ref, sin_ref, gh_ref, gl_ref, spec_ref):
    share, blocks, lanes = f_ref.shape
    cos, sin = cos_ref[...], sin_ref[...]
    rows = []
    for pair in range(share // 2):
        x = jnp.concatenate([f_ref[2 * pair], f_ref[2 * pair + 1]], axis=1)
        high, low = split(x)
        part = dot(into3_ref[...], jnp.concatenate([high, low, high], axis=0))
        rows.append(turned(part[:, :lanes], blocks, cos, sin))
        rows.append(turned(part[:, lanes:], blocks, cos, sin))
    high, low = split(jnp.concatenate(rows, axis=0))
    spec_ref[...] = across(high, low, gh_ref[...], gl_ref[...]) * scale


def conv_kernel(x_ref, filt_ref, into_ref, out_tab_ref, cos_ref, sin_ref, gh_ref, gl_ref, y_ref, spec_ref, wide_ref):
    blocks, fields, lanes = x_ref.shape
    share = fields // 2
    cos, sin = cos_ref[...], sin_ref[...]
    wide_ref[...] = x_ref[...].astype(F32).reshape(blocks * fields, lanes)
    rows = []
    for pair in range(fields // 2):
        x = jnp.concatenate(
            [wide_ref[pl.ds(2 * pair + one, blocks, stride=fields), :] for one in range(2)], axis=1
        ).astype(BF)
        part = dot(into_ref[...], jnp.concatenate([x, x], axis=0))
        rows.append(turned(part[:, :lanes], blocks, cos, sin))
        rows.append(turned(part[:, lanes:], blocks, cos, sin))
    high, low = split(jnp.concatenate(rows, axis=0))
    spec_ref[...] = across(high, low, gh_ref[...], gl_ref[...])
    half = share * blocks
    fr, fi = filt_ref[:, :lanes], filt_ref[:, lanes:]
    xr, xi = spec_ref[:half, :lanes], spec_ref[:half, lanes:]
    gr, gi = spec_ref[half:, :lanes], spec_ref[half:, lanes:]
    conv = jnp.concatenate([fr * xi + fi * xr, fr * xr - fi * xi], axis=1)
    back = jnp.concatenate([fr * gi - fi * gr, fr * gr + fi * gi], axis=1)
    high, low = split(jnp.concatenate([conv, back], axis=0))
    inner = across(high, low, gh_ref[...], gl_ref[...])
    ys = back_to_positions(inner, out_tab_ref, cos, sin, blocks, lanes)
    for f, y in enumerate(ys):
        wide_ref[pl.ds(f, blocks, stride=fields), :] = y
    y_ref[...] = wide_ref[...].reshape(blocks, fields, lanes).astype(BF)


def taps_kernel(scale, spec_ref, out_tab_ref, cos_ref, sin_ref, gh_ref, gl_ref, taps_ref, wide_ref):
    blocks, lanes = cos_ref.shape
    half = spec_ref.shape[0] // 2
    share = half // blocks
    cos, sin = cos_ref[...], sin_ref[...]
    xr, xi = spec_ref[:half, :lanes], spec_ref[:half, lanes:]
    gr, gi = spec_ref[half:, :lanes], spec_ref[half:, lanes:]
    prod = jnp.concatenate([xr * gi - xi * gr, xr * gr + xi * gi], axis=1)
    high, low = split(prod * scale)
    inner = across(high, low, gh_ref[...], gl_ref[...])
    for c, y in enumerate(back_to_positions(inner, out_tab_ref, cos, sin, blocks, lanes)):
        wide_ref[pl.ds(c, blocks, stride=share), :] = y
    taps_ref[...] = wide_ref[...].astype(BF)


def mix_kernel(q_hbm, k_hbm, v_hbm, g_hbm, out_ref, q_ref, k_ref, v_ref, g_ref, sems):
    groups, fields, lanes = out_ref.shape
    share = fields // 2
    copies = [
        pltpu.make_async_copy(source, target, sems.at[i])
        for i, (source, target) in enumerate(
            [(k_hbm, k_ref), (v_hbm, v_ref), (g_hbm, g_ref), (q_hbm, q_ref)]
        )
    ]
    for copy in copies:
        copy.start()

    def turn(a, b):
        prod = (a[0].astype(F32) * b[0].astype(F32)).astype(BF).astype(F32)
        return prod.T.reshape(groups, share, lanes)

    copies[0].wait()
    copies[1].wait()
    mixed = turn(k_ref, v_ref)
    copies[2].wait()
    copies[3].wait()
    out_ref[...] = jnp.concatenate([mixed, turn(g_ref, q_ref)], axis=1).astype(BF)


def gate_kernel(y_ref, mine_ref, other_ref, q_ref, k_ref, v_ref, g_ref, go_ref, gq_ref, gk_ref, gv_ref, taps_ref):
    taps_ref[...] = mine_ref[...].astype(F32) + other_ref[...].astype(F32)
    groups, fields, lanes = y_ref.shape
    share = fields // 2
    both = y_ref[...].astype(F32)
    conv = both[:, :share].reshape(groups * share, lanes).T
    back = both[:, share:].reshape(groups * share, lanes).T
    go_ref[0] = (q_ref[0].astype(F32) * conv).astype(BF)
    gq_ref[0] = (g_ref[0].astype(F32) * conv).astype(BF)
    gk_ref[0] = (back * v_ref[0].astype(F32)).astype(BF)
    gv_ref[0] = (back * k_ref[0].astype(F32)).astype(BF)


PARAMS = pltpu.CompilerParams(vmem_limit_bytes=32 * 1024 * 1024)


def on_device(query_proj, key_proj, value_proj, long_filter, grad_output):
    tok_count = query_proj.shape[1]
    width = query_proj.shape[2]
    groups = lax.axis_size("ctx")
    seqs = lax.axis_size("dp")
    seq_len = tok_count * groups
    share = width // groups
    t = make_tables(groups, tok_count)
    spec_rows = share * groups

    both = pl.pallas_call(
        mix_kernel,
        out_shape=jax.ShapeDtypeStruct((groups, 2 * share, tok_count), BF),
        in_specs=[pl.BlockSpec(memory_space=pltpu.HBM)] * 4,
        scratch_shapes=[pltpu.VMEM(query_proj.shape, BF)] * 4 + [pltpu.SemaphoreType.DMA((4,))],
        compiler_params=pltpu.CompilerParams(vmem_limit_bytes=60 * 1024 * 1024),
    )(query_proj, key_proj, value_proj, grad_output)
    both = lax.all_to_all(both, "ctx", 0, 0)

    filt_spec = pl.pallas_call(
        lambda *refs: filter_kernel(2.0 / (2 * seq_len), *refs),
        out_shape=jax.ShapeDtypeStruct((spec_rows, 2 * tok_count), F32),
        compiler_params=PARAMS,
    )(long_filter.T.reshape(share, groups, tok_count), t["into3"], t["turn_cos"], t["turn_sin"], t["g_high"], t["g_low"])

    out, spec = pl.pallas_call(
        conv_kernel,
        out_shape=(
            jax.ShapeDtypeStruct((groups, 2 * share, tok_count), BF),
            jax.ShapeDtypeStruct((2 * spec_rows, 2 * tok_count), F32),
        ),
        scratch_shapes=[pltpu.VMEM((2 * spec_rows, tok_count), F32)],
        compiler_params=PARAMS,
    )(both, filt_spec, t["into"], t["out"], t["turn_cos"], t["turn_sin"], t["g_high"], t["g_low"])
    out = lax.all_to_all(out, "ctx", 0, 0)

    factor = 1.0 / math.sqrt(seq_len * seqs)
    taps = pl.pallas_call(
        lambda *refs: taps_kernel(factor * 2.0 / (2 * seq_len), *refs),
        out_shape=jax.ShapeDtypeStruct((spec_rows, tok_count), BF),
        scratch_shapes=[pltpu.VMEM((spec_rows, tok_count), F32)],
        compiler_params=PARAMS,
    )(spec, t["out"], t["turn_cos"], t["turn_sin"], t["g_high"], t["g_low"])
    def swap(part, flip):
        return lax.ppermute(part, "dp", [(i, i ^ flip) for i in range(seqs)])

    def add(a, b):
        return (a.astype(F32) + b.astype(F32)).astype(BF)

    a, b, c = swap(taps, 2), swap(taps, 6), swap(taps, 4)
    taps = (taps.astype(F32) + c.astype(F32)) + (a.astype(F32) + b.astype(F32))
    taps = taps.astype(BF)
    other = swap(taps, 1)
    *grads, grad_filter = pl.pallas_call(
        gate_kernel,
        out_shape=[jax.ShapeDtypeStruct(query_proj.shape, BF)] * 4 + [jax.ShapeDtypeStruct(taps.shape, F32)],
        compiler_params=PARAMS,
    )(out, taps, other, query_proj, key_proj, value_proj, grad_output)
    grad_filter = grad_filter.reshape(groups, share, tok_count).transpose(0, 2, 1).reshape(seq_len, share)
    return (*grads, grad_filter)


def solution(mesh):
    tokens = P("dp", "ctx", None)
    taps = P(None, "ctx")
    return jax.shard_map(
        on_device,
        mesh=mesh,
        in_specs=(tokens, tokens, tokens, taps, tokens),
        out_specs=(tokens, tokens, tokens, tokens, taps),
        check_vma=False,
    )
```

```python
import math

import jax
import jax.numpy as jnp
import ml_dtypes
import numpy as np
from jax import lax
from jax.experimental import pallas as pl
from jax.experimental.pallas import tpu as pltpu
from jax.sharding import PartitionSpec as P

BF = jnp.bfloat16
F32 = jnp.float32
CHUNK = 256


def halves(table):
    high = table.astype(np.float32).astype(ml_dtypes.bfloat16)
    low = (table - high.astype(np.float64)).astype(np.float32).astype(ml_dtypes.bfloat16)
    return high, low


def make_tables(blocks, lanes):
    period = 2 * blocks
    total = period * lanes
    n = np.arange(blocks)
    odd = 2 * np.arange(blocks) + 1
    angle = math.pi / period * (n[None, :] * odd[:, None] % (2 * period))
    first = np.concatenate([np.cos(angle), -np.sin(angle)])
    m = np.arange(lanes)
    turn = math.pi / total * (odd[:, None] * m[None, :] % (2 * total))
    angle = 2 * math.pi / lanes * (m[:, None] * m[None, :] % lanes)
    cos, sin = np.cos(angle), np.sin(angle)
    second = np.block([[cos, -sin], [sin, cos]])
    a_high, a_low = halves(first)
    b_high, b_low = halves(first.T)
    g_high, g_low = halves(second)
    return dict(
        into=np.concatenate([a_high, a_low], axis=1),
        into3=np.concatenate([a_high, a_high, a_low], axis=1),
        out=np.block([[b_high, b_high], [b_low, np.zeros_like(b_low)]]),
        turn_cos=np.cos(turn).astype(np.float32),
        turn_sin=np.sin(turn).astype(np.float32),
        g_high=g_high,
        g_low=g_low,
    )


def dot(a, b):
    return jnp.dot(a, b, preferred_element_type=F32)


def split(x):
    high = x.astype(BF)
    return high, (x - high.astype(F32)).astype(BF)


def across(z_high, z_low, g_high, g_low):
    return dot(z_high, g_high) + dot(z_low, g_high) + dot(z_high, g_low)


def turned(part, blocks, cos, sin):
    re, im = part[:blocks], part[blocks:]
    return jnp.concatenate([re * cos + im * sin, im * cos - re * sin], axis=1)


def back_to_positions(spec, out_ref, cos, sin, blocks, lanes):
    count = spec.shape[0] // blocks
    result = []
    for pair in range(count // 2):
        rows = []
        for one in range(2):
            c = 2 * pair + one
            block = spec[c * blocks:(c + 1) * blocks]
            im, re = block[:, :lanes], block[:, lanes:]
            rows.append(jnp.concatenate([re * cos - im * sin, im * cos + re * sin], axis=0))
        both = jnp.concatenate(rows, axis=1)
        high, low = split(both)
        y = dot(out_ref[...], jnp.concatenate([high, low], axis=0))
        y = y[:blocks] + y[blocks:]
        result += [y[:, :lanes], y[:, lanes:]]
    return result


def filter_kernel(scale, f_ref, into3_ref, cos_ref, sin_ref, gh_ref, gl_ref, spec_ref):
    share, blocks, lanes = f_ref.shape
    cos, sin = cos_ref[...], sin_ref[...]
    rows = []
    for pair in range(share // 2):
        x = jnp.concatenate([f_ref[2 * pair], f_ref[2 * pair + 1]], axis=1)
        high, low = split(x)
        part = dot(into3_ref[...], jnp.concatenate([high, low, high], axis=0))
        rows.append(turned(part[:, :lanes], blocks, cos, sin))
        rows.append(turned(part[:, lanes:], blocks, cos, sin))
    high, low = split(jnp.concatenate(rows, axis=0))
    spec_ref[...] = across(high, low, gh_ref[...], gl_ref[...]) * scale


def conv_kernel(
    scale, x_ref, filt_ref, into_ref, out_tab_ref, cos_ref, sin_ref, gh_ref, gl_ref,
    y_ref, taps_ref, wide_ref, wide_taps_ref, high_ref, low_ref, spec_ref, inner_ref,
):
    blocks, fields, lanes = x_ref.shape
    share = fields // 2
    step = 2 * blocks
    half = share // 2
    cos, sin = cos_ref[...], sin_ref[...]
    wide_ref[...] = x_ref[...].astype(F32).reshape(blocks * fields, lanes)

    def put(i, parts):
        high, low = split(jnp.concatenate(parts, axis=1))
        high_ref[i * step:(i + 1) * step] = high
        low_ref[i * step:(i + 1) * step] = low

    def transform(count, out_ref):
        for start in range(0, count * step, CHUNK):
            rows = slice(start, min(start + CHUNK, count * step))
            out_ref[rows] = across(high_ref[rows], low_ref[rows], gh_ref[...], gl_ref[...])

    for i in range(share):
        x = jnp.concatenate(
            [wide_ref[pl.ds(2 * i + one, blocks, stride=fields), :] for one in range(2)], axis=1
        ).astype(BF)
        part = dot(into_ref[...], jnp.concatenate([x, x], axis=0))
        turns = [turned(part[:, one * lanes:(one + 1) * lanes], blocks, cos, sin) for one in range(2)]
        put(i, [jnp.concatenate(turns, axis=0)])
    transform(share, spec_ref)
    for i in range(half):
        xs = spec_ref[i * step:(i + 1) * step]
        gs = spec_ref[(half + i) * step:(half + i + 1) * step]
        fs = filt_ref[i * step:(i + 1) * step]
        xr, xi, gr, gi = xs[:, :lanes], xs[:, lanes:], gs[:, :lanes], gs[:, lanes:]
        fr, fi = fs[:, :lanes], fs[:, lanes:]
        put(i, [fr * xi + fi * xr, fr * xr - fi * xi])
        put(half + i, [fr * gi - fi * gr, fr * gr + fi * gi])
        put(share + i, [scale * (xr * gi - xi * gr), scale * (xr * gr + xi * gi)])
    transform(share + half, inner_ref)
    for i in range(share + half):
        inner = inner_ref[i * step:(i + 1) * step]
        for one, y in enumerate(back_to_positions(inner, out_tab_ref, cos, sin, blocks, lanes)):
            field = 2 * i + one
            if field < fields:
                wide_ref[pl.ds(field, blocks, stride=fields), :] = y
            else:
                wide_taps_ref[pl.ds(field - fields, blocks, stride=share), :] = y
    y_ref[...] = wide_ref[...].reshape(blocks, fields, lanes).astype(BF)
    taps_ref[...] = wide_taps_ref[...].astype(BF)


def mix_kernel(q_hbm, k_hbm, v_hbm, g_hbm, out_ref, q_ref, k_ref, v_ref, g_ref, sems):
    groups, fields, lanes = out_ref.shape
    share = fields // 2
    copies = [
        pltpu.make_async_copy(source, target, sems.at[i])
        for i, (source, target) in enumerate(
            [(k_hbm, k_ref), (v_hbm, v_ref), (g_hbm, g_ref), (q_hbm, q_ref)]
        )
    ]
    for copy in copies:
        copy.start()

    def turn(a, b):
        prod = (a[0].astype(F32) * b[0].astype(F32)).astype(BF).astype(F32)
        return prod.T.reshape(groups, share, lanes)

    copies[0].wait()
    copies[1].wait()
    mixed = turn(k_ref, v_ref)
    copies[2].wait()
    copies[3].wait()
    out_ref[...] = jnp.concatenate([mixed, turn(g_ref, q_ref)], axis=1).astype(BF)


def gate_kernel(y_ref, mine_ref, other_ref, q_ref, k_ref, v_ref, g_ref, go_ref, gq_ref, gk_ref, gv_ref, taps_ref):
    taps_ref[...] = mine_ref[...].astype(F32) + other_ref[...].astype(F32)
    groups, fields, lanes = y_ref.shape
    share = fields // 2
    both = y_ref[...].astype(F32)
    conv = both[:, :share].reshape(groups * share, lanes).T
    back = both[:, share:].reshape(groups * share, lanes).T
    go_ref[0] = (q_ref[0].astype(F32) * conv).astype(BF)
    gq_ref[0] = (g_ref[0].astype(F32) * conv).astype(BF)
    gk_ref[0] = (back * v_ref[0].astype(F32)).astype(BF)
    gv_ref[0] = (back * k_ref[0].astype(F32)).astype(BF)


PARAMS = pltpu.CompilerParams(vmem_limit_bytes=32 * 1024 * 1024)


def on_device(query_proj, key_proj, value_proj, long_filter, grad_output):
    tok_count = query_proj.shape[1]
    width = query_proj.shape[2]
    groups = lax.axis_size("ctx")
    seqs = lax.axis_size("dp")
    seq_len = tok_count * groups
    share = width // groups
    t = make_tables(groups, tok_count)
    spec_rows = share * groups

    both = pl.pallas_call(
        mix_kernel,
        out_shape=jax.ShapeDtypeStruct((groups, 2 * share, tok_count), BF),
        in_specs=[pl.BlockSpec(memory_space=pltpu.HBM)] * 4,
        scratch_shapes=[pltpu.VMEM(query_proj.shape, BF)] * 4 + [pltpu.SemaphoreType.DMA((4,))],
        compiler_params=pltpu.CompilerParams(vmem_limit_bytes=60 * 1024 * 1024),
    )(query_proj, key_proj, value_proj, grad_output)
    both = lax.all_to_all(both, "ctx", 0, 0)

    filt_spec = pl.pallas_call(
        lambda *refs: filter_kernel(2.0 / (2 * seq_len), *refs),
        out_shape=jax.ShapeDtypeStruct((spec_rows, 2 * tok_count), F32),
        compiler_params=PARAMS,
    )(long_filter.T.reshape(share, groups, tok_count), t["into3"], t["turn_cos"], t["turn_sin"], t["g_high"], t["g_low"])

    factor = 1.0 / math.sqrt(seq_len * seqs)
    out, taps = pl.pallas_call(
        lambda *refs: conv_kernel(factor * 2.0 / (2 * seq_len), *refs),
        out_shape=(
            jax.ShapeDtypeStruct((groups, 2 * share, tok_count), BF),
            jax.ShapeDtypeStruct((spec_rows, tok_count), BF),
        ),
        scratch_shapes=[
            pltpu.VMEM((2 * spec_rows, tok_count), F32),
            pltpu.VMEM((spec_rows, tok_count), F32),
            pltpu.VMEM((3 * spec_rows, 2 * tok_count), BF),
            pltpu.VMEM((3 * spec_rows, 2 * tok_count), BF),
            pltpu.VMEM((2 * spec_rows, 2 * tok_count), F32),
            pltpu.VMEM((3 * spec_rows, 2 * tok_count), F32),
        ],
        compiler_params=PARAMS,
    )(both, filt_spec, t["into"], t["out"], t["turn_cos"], t["turn_sin"], t["g_high"], t["g_low"])
    out = lax.all_to_all(out, "ctx", 0, 0)

    def swap(part, flip):
        return lax.ppermute(part, "dp", [(i, i ^ flip) for i in range(seqs)])

    def add(a, b):
        return (a.astype(F32) + b.astype(F32)).astype(BF)

    a, b, c = swap(taps, 2), swap(taps, 6), swap(taps, 4)
    taps = (taps.astype(F32) + c.astype(F32)) + (a.astype(F32) + b.astype(F32))
    taps = taps.astype(BF)
    other = swap(taps, 1)
    *grads, grad_filter = pl.pallas_call(
        gate_kernel,
        out_shape=[jax.ShapeDtypeStruct(query_proj.shape, BF)] * 4 + [jax.ShapeDtypeStruct(taps.shape, F32)],
        compiler_params=PARAMS,
    )(out, taps, other, query_proj, key_proj, value_proj, grad_output)
    grad_filter = grad_filter.reshape(groups, share, tok_count).transpose(0, 2, 1).reshape(seq_len, share)
    return (*grads, grad_filter)


def solution(mesh):
    tokens = P("dp", "ctx", None)
    taps = P(None, "ctx")
    return jax.shard_map(
        on_device,
        mesh=mesh,
        in_specs=(tokens, tokens, tokens, taps, tokens),
        out_specs=(tokens, tokens, tokens, tokens, taps),
        check_vma=False,
    )
```

```python
import math

import jax
import jax.numpy as jnp
import ml_dtypes
import numpy as np
from jax import lax
from jax.experimental import pallas as pl
from jax.experimental.pallas import tpu as pltpu
from jax.sharding import PartitionSpec as P

BF = jnp.bfloat16
F32 = jnp.float32
CHUNK = 256
PLANE = 4


def halves(table):
    high = table.astype(np.float32).astype(ml_dtypes.bfloat16)
    low = (table - high.astype(np.float64)).astype(np.float32).astype(ml_dtypes.bfloat16)
    return high, low


def spread(groups):
    planes = groups // PLANE
    bits = planes.bit_length() - 1
    reverse = [int(format(z, f"0{bits}b")[::-1], 2) for z in range(planes)]
    return [z * PLANE + one for z in reverse for one in range(PLANE)]


def make_tables(blocks, lanes):
    order = spread(blocks)
    period = 2 * blocks
    total = period * lanes
    n = np.arange(blocks)
    odd = 2 * np.arange(blocks) + 1
    angle = math.pi / period * (n[None, :] * odd[:, None] % (2 * period))
    first = np.concatenate([np.cos(angle), -np.sin(angle)])
    m = np.arange(lanes)
    turn = math.pi / total * (odd[:, None] * m[None, :] % (2 * total))
    angle = 2 * math.pi / lanes * (m[:, None] * m[None, :] % lanes)
    cos, sin = np.cos(angle), np.sin(angle)
    second = np.block([[cos, -sin], [sin, cos]])
    a_high, a_low = halves(first)
    b_high, b_low = halves(first.T)
    g_high, g_low = halves(second)
    return dict(
        into=np.concatenate([a_high, a_low], axis=1)[:, order + [blocks + n for n in order]],
        into3=np.concatenate([a_high, a_high, a_low], axis=1),
        out=np.block([[b_high, b_high], [b_low, np.zeros_like(b_low)]]),
        turn_cos=np.cos(turn).astype(np.float32),
        turn_sin=np.sin(turn).astype(np.float32),
        g_high=g_high,
        g_low=g_low,
    )


def dot(a, b):
    return jnp.dot(a, b, preferred_element_type=F32)


def split(x):
    high = x.astype(BF)
    return high, (x - high.astype(F32)).astype(BF)


def across(z_high, z_low, g_high, g_low):
    return dot(z_high, g_high) + dot(z_low, g_high) + dot(z_high, g_low)


def turned(part, blocks, cos, sin):
    re, im = part[:blocks], part[blocks:]
    return jnp.concatenate([re * cos + im * sin, im * cos - re * sin], axis=1)


def back_to_positions(spec, out_ref, cos, sin, blocks, lanes):
    count = spec.shape[0] // blocks
    result = []
    for pair in range(count // 2):
        rows = []
        for one in range(2):
            c = 2 * pair + one
            block = spec[c * blocks:(c + 1) * blocks]
            im, re = block[:, :lanes], block[:, lanes:]
            rows.append(jnp.concatenate([re * cos - im * sin, im * cos + re * sin], axis=0))
        both = jnp.concatenate(rows, axis=1)
        high, low = split(both)
        y = dot(out_ref[...], jnp.concatenate([high, low], axis=0))
        y = y[:blocks] + y[blocks:]
        result += [y[:, :lanes], y[:, lanes:]]
    return result


def filter_kernel(scale, f_ref, into3_ref, cos_ref, sin_ref, gh_ref, gl_ref, spec_ref):
    share, blocks, lanes = f_ref.shape
    cos, sin = cos_ref[...], sin_ref[...]
    rows = []
    for pair in range(share // 2):
        x = jnp.concatenate([f_ref[2 * pair], f_ref[2 * pair + 1]], axis=1)
        high, low = split(x)
        part = dot(into3_ref[...], jnp.concatenate([high, low, high], axis=0))
        rows.append(turned(part[:, :lanes], blocks, cos, sin))
        rows.append(turned(part[:, lanes:], blocks, cos, sin))
    high, low = split(jnp.concatenate(rows, axis=0))
    spec_ref[...] = across(high, low, gh_ref[...], gl_ref[...]) * scale


def conv_kernel(
    scale, x_ref, filt_ref, into_ref, out_tab_ref, cos_ref, sin_ref, gh_ref, gl_ref,
    y_ref, taps_ref, wide_ref, wide_taps_ref, high_ref, low_ref, spec_ref, inner_ref,
):
    blocks, fields, lanes = x_ref.shape
    share = fields // 2
    step = 2 * blocks
    half = share // 2
    cos, sin = cos_ref[...], sin_ref[...]
    wide_ref[...] = x_ref[...].astype(F32).reshape(blocks * fields, lanes)

    def put(i, parts):
        high, low = split(jnp.concatenate(parts, axis=1))
        high_ref[i * step:(i + 1) * step] = high
        low_ref[i * step:(i + 1) * step] = low

    def transform(count, out_ref):
        for start in range(0, count * step, CHUNK):
            rows = slice(start, min(start + CHUNK, count * step))
            out_ref[rows] = across(high_ref[rows], low_ref[rows], gh_ref[...], gl_ref[...])

    for i in range(share):
        x = jnp.concatenate(
            [wide_ref[pl.ds(2 * i + one, blocks, stride=fields), :] for one in range(2)], axis=1
        ).astype(BF)
        part = dot(into_ref[...], jnp.concatenate([x, x], axis=0))
        turns = [turned(part[:, one * lanes:(one + 1) * lanes], blocks, cos, sin) for one in range(2)]
        put(i, [jnp.concatenate(turns, axis=0)])
    transform(share, spec_ref)
    for i in range(half):
        xs = spec_ref[i * step:(i + 1) * step]
        gs = spec_ref[(half + i) * step:(half + i + 1) * step]
        fs = filt_ref[i * step:(i + 1) * step]
        xr, xi, gr, gi = xs[:, :lanes], xs[:, lanes:], gs[:, :lanes], gs[:, lanes:]
        fr, fi = fs[:, :lanes], fs[:, lanes:]
        put(i, [fr * xi + fi * xr, fr * xr - fi * xi])
        put(half + i, [fr * gi - fi * gr, fr * gr + fi * gi])
        put(share + i, [scale * (xr * gi - xi * gr), scale * (xr * gr + xi * gi)])
    transform(share + half, inner_ref)
    for i in range(share + half):
        inner = inner_ref[i * step:(i + 1) * step]
        for one, y in enumerate(back_to_positions(inner, out_tab_ref, cos, sin, blocks, lanes)):
            field = 2 * i + one
            if field < fields:
                wide_ref[pl.ds(field, blocks, stride=fields), :] = y
            else:
                wide_taps_ref[pl.ds(field - fields, blocks, stride=share), :] = y
    y_ref[...] = wide_ref[...].reshape(blocks, fields, lanes).astype(BF)
    taps_ref[...] = wide_taps_ref[...].astype(BF)


def mix_kernel(q_hbm, k_hbm, v_hbm, g_hbm, out_ref, q_ref, k_ref, v_ref, g_ref, sems):
    groups, fields, lanes = out_ref.shape
    share = fields // 2
    copies = [
        pltpu.make_async_copy(source, target, sems.at[i])
        for i, (source, target) in enumerate(
            [(k_hbm, k_ref), (v_hbm, v_ref), (g_hbm, g_ref), (q_hbm, q_ref)]
        )
    ]
    for copy in copies:
        copy.start()

    def turn(a, b):
        prod = (a[0].astype(F32) * b[0].astype(F32)).astype(BF).astype(F32)
        return prod.T.reshape(groups, share, lanes)

    copies[0].wait()
    copies[1].wait()
    mixed = turn(k_ref, v_ref)
    copies[2].wait()
    copies[3].wait()
    both = jnp.concatenate([mixed, turn(g_ref, q_ref)], axis=1).astype(BF)
    for place, group in enumerate(spread(groups)[::PLANE]):
        out_ref[place * PLANE:(place + 1) * PLANE] = both[group:group + PLANE]


def gate_kernel(y_ref, mine_ref, other_ref, q_ref, k_ref, v_ref, g_ref, go_ref, gq_ref, gk_ref, gv_ref, taps_ref):
    taps_ref[...] = mine_ref[...].astype(F32) + other_ref[...].astype(F32)
    groups, fields, lanes = y_ref.shape
    share = fields // 2
    both = y_ref[...].astype(F32)
    conv = both[:, :share].reshape(groups * share, lanes).T
    back = both[:, share:].reshape(groups * share, lanes).T
    go_ref[0] = (q_ref[0].astype(F32) * conv).astype(BF)
    gq_ref[0] = (g_ref[0].astype(F32) * conv).astype(BF)
    gk_ref[0] = (back * v_ref[0].astype(F32)).astype(BF)
    gv_ref[0] = (back * k_ref[0].astype(F32)).astype(BF)


PARAMS = pltpu.CompilerParams(vmem_limit_bytes=32 * 1024 * 1024)


def on_device(query_proj, key_proj, value_proj, long_filter, grad_output):
    tok_count = query_proj.shape[1]
    width = query_proj.shape[2]
    groups = lax.axis_size("ctx")
    seqs = lax.axis_size("dp")
    seq_len = tok_count * groups
    share = width // groups
    t = make_tables(groups, tok_count)
    spec_rows = share * groups

    both = pl.pallas_call(
        mix_kernel,
        out_shape=jax.ShapeDtypeStruct((groups, 2 * share, tok_count), BF),
        in_specs=[pl.BlockSpec(memory_space=pltpu.HBM)] * 4,
        scratch_shapes=[pltpu.VMEM(query_proj.shape, BF)] * 4 + [pltpu.SemaphoreType.DMA((4,))],
        compiler_params=pltpu.CompilerParams(vmem_limit_bytes=60 * 1024 * 1024),
    )(query_proj, key_proj, value_proj, grad_output)
    both = lax.all_to_all(both, "ctx", 0, 0, axis_index_groups=[spread(groups)])

    filt_spec = pl.pallas_call(
        lambda *refs: filter_kernel(2.0 / (2 * seq_len), *refs),
        out_shape=jax.ShapeDtypeStruct((spec_rows, 2 * tok_count), F32),
        compiler_params=PARAMS,
    )(long_filter.T.reshape(share, groups, tok_count), t["into3"], t["turn_cos"], t["turn_sin"], t["g_high"], t["g_low"])

    factor = 1.0 / math.sqrt(seq_len * seqs)
    out, taps = pl.pallas_call(
        lambda *refs: conv_kernel(factor * 2.0 / (2 * seq_len), *refs),
        out_shape=(
            jax.ShapeDtypeStruct((groups, 2 * share, tok_count), BF),
            jax.ShapeDtypeStruct((spec_rows, tok_count), BF),
        ),
        scratch_shapes=[
            pltpu.VMEM((2 * spec_rows, tok_count), F32),
            pltpu.VMEM((spec_rows, tok_count), F32),
            pltpu.VMEM((3 * spec_rows, 2 * tok_count), BF),
            pltpu.VMEM((3 * spec_rows, 2 * tok_count), BF),
            pltpu.VMEM((2 * spec_rows, 2 * tok_count), F32),
            pltpu.VMEM((3 * spec_rows, 2 * tok_count), F32),
        ],
        compiler_params=PARAMS,
    )(both, filt_spec, t["into"], t["out"], t["turn_cos"], t["turn_sin"], t["g_high"], t["g_low"])
    out = lax.all_to_all(out, "ctx", 0, 0)

    def swap(part, flip):
        return lax.ppermute(part, "dp", [(i, i ^ flip) for i in range(seqs)])

    def add(a, b):
        return (a.astype(F32) + b.astype(F32)).astype(BF)

    a, b, c = swap(taps, 2), swap(taps, 6), swap(taps, 4)
    taps = (taps.astype(F32) + c.astype(F32)) + (a.astype(F32) + b.astype(F32))
    taps = taps.astype(BF)
    other = swap(taps, 1)
    *grads, grad_filter = pl.pallas_call(
        gate_kernel,
        out_shape=[jax.ShapeDtypeStruct(query_proj.shape, BF)] * 4 + [jax.ShapeDtypeStruct(taps.shape, F32)],
        compiler_params=PARAMS,
    )(out, taps, other, query_proj, key_proj, value_proj, grad_output)
    grad_filter = grad_filter.reshape(groups, share, tok_count).transpose(0, 2, 1).reshape(seq_len, share)
    return (*grads, grad_filter)


def solution(mesh):
    tokens = P("dp", "ctx", None)
    taps = P(None, "ctx")
    return jax.shard_map(
        on_device,
        mesh=mesh,
        in_specs=(tokens, tokens, tokens, taps, tokens),
        out_specs=(tokens, tokens, tokens, tokens, taps),
        check_vma=False,
    )
```

```python
import math

import jax
import jax.numpy as jnp
import ml_dtypes
import numpy as np
from jax import lax
from jax.experimental import pallas as pl
from jax.experimental.pallas import tpu as pltpu
from jax.sharding import PartitionSpec as P

BF = jnp.bfloat16
F32 = jnp.float32
CHUNK = 256
PLANE = 4


def halves(table):
    high = table.astype(np.float32).astype(ml_dtypes.bfloat16)
    low = (table - high.astype(np.float64)).astype(np.float32).astype(ml_dtypes.bfloat16)
    return high, low


def spread(groups):
    planes = groups // PLANE
    bits = planes.bit_length() - 1
    reverse = [int(format(z, f"0{bits}b")[::-1], 2) for z in range(planes)]
    return [z * PLANE + one for z in reverse for one in range(PLANE)]


def make_tables(blocks, lanes):
    order = spread(blocks)
    period = 2 * blocks
    total = period * lanes
    n = np.arange(blocks)
    odd = 2 * np.arange(blocks) + 1
    angle = math.pi / period * (n[None, :] * odd[:, None] % (2 * period))
    first = np.concatenate([np.cos(angle), -np.sin(angle)])
    m = np.arange(lanes)
    turn = math.pi / total * (odd[:, None] * m[None, :] % (2 * total))
    angle = 2 * math.pi / lanes * (m[:, None] * m[None, :] % lanes)
    cos, sin = np.cos(angle), np.sin(angle)
    second = np.block([[cos, -sin], [sin, cos]])
    a_high, a_low = halves(first)
    b_high, b_low = halves(first.T)
    g_high, g_low = halves(second)
    return dict(
        into=np.concatenate([a_high, a_low], axis=1)[:, order + [blocks + n for n in order]],
        into3=np.concatenate([a_high, a_high, a_low], axis=1),
        out=np.block([[b_high, b_high], [b_low, np.zeros_like(b_low)]]),
        turn_cos=np.cos(turn).astype(np.float32),
        turn_sin=np.sin(turn).astype(np.float32),
        g_high=g_high,
        g_low=g_low,
    )


def dot(a, b):
    return jnp.dot(a, b, preferred_element_type=F32)


def split(x):
    high = x.astype(BF)
    return high, (x - high.astype(F32)).astype(BF)


def across(z_high, z_low, g_high, g_low):
    return dot(z_high, g_high) + dot(z_low, g_high) + dot(z_high, g_low)


def turned(part, blocks, cos, sin):
    re, im = part[:blocks], part[blocks:]
    return jnp.concatenate([re * cos + im * sin, im * cos - re * sin], axis=1)


def back_to_positions(spec, out_ref, cos, sin, blocks, lanes):
    count = spec.shape[0] // blocks
    result = []
    for pair in range(count // 2):
        rows = []
        for one in range(2):
            c = 2 * pair + one
            block = spec[c * blocks:(c + 1) * blocks]
            im, re = block[:, :lanes], block[:, lanes:]
            rows.append(jnp.concatenate([re * cos - im * sin, im * cos + re * sin], axis=0))
        both = jnp.concatenate(rows, axis=1)
        high, low = split(both)
        y = dot(out_ref[...], jnp.concatenate([high, low], axis=0))
        y = y[:blocks] + y[blocks:]
        result += [y[:, :lanes], y[:, lanes:]]
    return result


def filter_kernel(scale, f_ref, into3_ref, cos_ref, sin_ref, gh_ref, gl_ref, spec_ref):
    share, blocks, lanes = f_ref.shape
    cos, sin = cos_ref[...], sin_ref[...]
    rows = []
    for pair in range(share // 2):
        x = jnp.concatenate([f_ref[2 * pair], f_ref[2 * pair + 1]], axis=1)
        high, low = split(x)
        part = dot(into3_ref[...], jnp.concatenate([high, low, high], axis=0))
        rows.append(turned(part[:, :lanes], blocks, cos, sin))
        rows.append(turned(part[:, lanes:], blocks, cos, sin))
    high, low = split(jnp.concatenate(rows, axis=0))
    spec_ref[...] = across(high, low, gh_ref[...], gl_ref[...]) * scale


def conv_kernel(
    scale, x_ref, filt_ref, into_ref, out_tab_ref, cos_ref, sin_ref, gh_ref, gl_ref,
    y_ref, taps_ref, wide_ref, wide_taps_ref, high_ref, low_ref, spec_ref, inner_ref,
):
    blocks, fields, lanes = x_ref.shape
    share = fields // 2
    step = 2 * blocks
    half = share // 2
    cos, sin = cos_ref[...], sin_ref[...]
    wide_ref[...] = x_ref[...].astype(F32).reshape(blocks * fields, lanes)

    def put(i, parts):
        high, low = split(jnp.concatenate(parts, axis=1))
        high_ref[i * step:(i + 1) * step] = high
        low_ref[i * step:(i + 1) * step] = low

    def transform(count, out_ref):
        for start in range(0, count * step, CHUNK):
            rows = slice(start, min(start + CHUNK, count * step))
            out_ref[rows] = across(high_ref[rows], low_ref[rows], gh_ref[...], gl_ref[...])

    for i in range(share):
        x = jnp.concatenate(
            [wide_ref[pl.ds(2 * i + one, blocks, stride=fields), :] for one in range(2)], axis=1
        ).astype(BF)
        part = dot(into_ref[...], jnp.concatenate([x, x], axis=0))
        turns = [turned(part[:, one * lanes:(one + 1) * lanes], blocks, cos, sin) for one in range(2)]
        put(i, [jnp.concatenate(turns, axis=0)])
    transform(share, spec_ref)
    for i in range(half):
        xs = spec_ref[i * step:(i + 1) * step]
        gs = spec_ref[(half + i) * step:(half + i + 1) * step]
        fs = filt_ref[i * step:(i + 1) * step]
        xr, xi, gr, gi = xs[:, :lanes], xs[:, lanes:], gs[:, :lanes], gs[:, lanes:]
        fr, fi = fs[:, :lanes], fs[:, lanes:]
        put(i, [fr * xi + fi * xr, fr * xr - fi * xi])
        put(half + i, [fr * gi - fi * gr, fr * gr + fi * gi])
        put(share + i, [scale * (xr * gi - xi * gr), scale * (xr * gr + xi * gi)])
    transform(share + half, inner_ref)
    for i in range(share + half):
        inner = inner_ref[i * step:(i + 1) * step]
        for one, y in enumerate(back_to_positions(inner, out_tab_ref, cos, sin, blocks, lanes)):
            field = 2 * i + one
            if field < fields:
                wide_ref[pl.ds(field, blocks, stride=fields), :] = y
            else:
                wide_taps_ref[pl.ds(field - fields, blocks, stride=share), :] = y
    y_ref[...] = wide_ref[...].reshape(blocks, fields, lanes).astype(BF)
    taps_ref[...] = wide_taps_ref[...].astype(BF)


def mix_kernel(q_hbm, k_hbm, v_hbm, g_hbm, out_ref, q_ref, k_ref, v_ref, g_ref, sems):
    groups, fields, lanes = out_ref.shape
    share = fields // 2
    copies = [
        pltpu.make_async_copy(source, target, sems.at[i])
        for i, (source, target) in enumerate(
            [(k_hbm, k_ref), (v_hbm, v_ref), (g_hbm, g_ref), (q_hbm, q_ref)]
        )
    ]
    for copy in copies:
        copy.start()

    def turn(a, b):
        prod = (a[0].astype(F32) * b[0].astype(F32)).astype(BF).astype(F32)
        return prod.T.reshape(groups, share, lanes)

    copies[0].wait()
    copies[1].wait()
    mixed = turn(k_ref, v_ref)
    copies[2].wait()
    copies[3].wait()
    both = jnp.concatenate([mixed, turn(g_ref, q_ref)], axis=1).astype(BF)
    for place, group in enumerate(spread(groups)[::PLANE]):
        out_ref[place * PLANE:(place + 1) * PLANE] = both[group:group + PLANE]


def gate_kernel(y_ref, mine_ref, other_ref, q_ref, k_ref, v_ref, g_ref, go_ref, gq_ref, gk_ref, gv_ref, taps_ref):
    taps_ref[...] = mine_ref[...].astype(F32) + other_ref[...].astype(F32)
    groups, fields, lanes = y_ref.shape
    share = fields // 2
    both = y_ref[...].astype(F32)
    conv = both[:, :share].reshape(groups * share, lanes).T
    back = both[:, share:].reshape(groups * share, lanes).T
    go_ref[0] = (q_ref[0].astype(F32) * conv).astype(BF)
    gq_ref[0] = (g_ref[0].astype(F32) * conv).astype(BF)
    gk_ref[0] = (back * v_ref[0].astype(F32)).astype(BF)
    gv_ref[0] = (back * k_ref[0].astype(F32)).astype(BF)


PARAMS = pltpu.CompilerParams(vmem_limit_bytes=32 * 1024 * 1024)


def on_device(query_proj, key_proj, value_proj, long_filter, grad_output):
    tok_count = query_proj.shape[1]
    width = query_proj.shape[2]
    groups = lax.axis_size("ctx")
    seqs = lax.axis_size("dp")
    seq_len = tok_count * groups
    share = width // groups
    t = make_tables(groups, tok_count)
    spec_rows = share * groups

    both = pl.pallas_call(
        mix_kernel,
        out_shape=jax.ShapeDtypeStruct((groups, 2 * share, tok_count), BF),
        in_specs=[pl.BlockSpec(memory_space=pltpu.HBM)] * 4,
        scratch_shapes=[pltpu.VMEM(query_proj.shape, BF)] * 4 + [pltpu.SemaphoreType.DMA((4,))],
        compiler_params=pltpu.CompilerParams(vmem_limit_bytes=60 * 1024 * 1024),
    )(query_proj, key_proj, value_proj, grad_output)
    both = lax.all_to_all(both, "ctx", 0, 0, axis_index_groups=[spread(groups)])

    filt_spec = pl.pallas_call(
        lambda *refs: filter_kernel(2.0 / (2 * seq_len), *refs),
        out_shape=jax.ShapeDtypeStruct((spec_rows, 2 * tok_count), F32),
        compiler_params=PARAMS,
    )(long_filter.T.reshape(share, groups, tok_count), t["into3"], t["turn_cos"], t["turn_sin"], t["g_high"], t["g_low"])

    factor = 1.0 / math.sqrt(seq_len * seqs)
    out, taps = pl.pallas_call(
        lambda *refs: conv_kernel(factor * 2.0 / (2 * seq_len), *refs),
        out_shape=(
            jax.ShapeDtypeStruct((groups, 2 * share, tok_count), BF),
            jax.ShapeDtypeStruct((spec_rows, tok_count), BF),
        ),
        scratch_shapes=[
            pltpu.VMEM((2 * spec_rows, tok_count), F32),
            pltpu.VMEM((spec_rows, tok_count), F32),
            pltpu.VMEM((3 * spec_rows, 2 * tok_count), BF),
            pltpu.VMEM((3 * spec_rows, 2 * tok_count), BF),
            pltpu.VMEM((2 * spec_rows, 2 * tok_count), F32),
            pltpu.VMEM((3 * spec_rows, 2 * tok_count), F32),
        ],
        compiler_params=PARAMS,
    )(both, filt_spec, t["into"], t["out"], t["turn_cos"], t["turn_sin"], t["g_high"], t["g_low"])
    out = lax.all_to_all(out, "ctx", 0, 0)

    def swap(part, flips):
        pairs = [
            (d * groups + c, (d ^ flips[c % 2]) * groups + c) for d in range(seqs) for c in range(groups)
        ]
        return lax.ppermute(part, ("dp", "ctx"), pairs)

    def add(a, b):
        return (a.astype(F32) + b.astype(F32)).astype(BF)

    taps = add(taps, swap(taps, (2, 6)))
    taps = add(taps, swap(taps, (6, 1)))
    other = swap(taps, (1, 2))

    *grads, grad_filter = pl.pallas_call(
        gate_kernel,
        out_shape=[jax.ShapeDtypeStruct(query_proj.shape, BF)] * 4 + [jax.ShapeDtypeStruct(taps.shape, F32)],
        compiler_params=PARAMS,
    )(out, taps, other, query_proj, key_proj, value_proj, grad_output)
    grad_filter = grad_filter.reshape(groups, share, tok_count).transpose(0, 2, 1).reshape(seq_len, share)
    return (*grads, grad_filter)


def solution(mesh):
    tokens = P("dp", "ctx", None)
    taps = P(None, "ctx")
    return jax.shard_map(
        on_device,
        mesh=mesh,
        in_specs=(tokens, tokens, tokens, taps, tokens),
        out_specs=(tokens, tokens, tokens, tokens, taps),
        check_vma=False,
    )
```

```python
import math

import jax
import jax.numpy as jnp
import ml_dtypes
import numpy as np
from jax import lax
from jax.experimental import pallas as pl
from jax.experimental.pallas import tpu as pltpu
from jax.sharding import PartitionSpec as P

BF = jnp.bfloat16
F32 = jnp.float32
CHUNK = 256
PLANE = 4


def halves(table):
    high = table.astype(np.float32).astype(ml_dtypes.bfloat16)
    low = (table - high.astype(np.float64)).astype(np.float32).astype(ml_dtypes.bfloat16)
    return high, low


def spread(groups):
    planes = groups // PLANE
    bits = planes.bit_length() - 1
    reverse = [(int(format(z, f"0{bits}b")[::-1], 2) + planes - 2) % planes for z in range(planes)]
    return [z * PLANE + one for z in reverse for one in range(PLANE)]


def make_tables(blocks, lanes):
    order = spread(blocks)
    period = 2 * blocks
    total = period * lanes
    n = np.arange(blocks)
    odd = 2 * np.arange(blocks) + 1
    angle = math.pi / period * (n[None, :] * odd[:, None] % (2 * period))
    first = np.concatenate([np.cos(angle), -np.sin(angle)])
    m = np.arange(lanes)
    turn = math.pi / total * (odd[:, None] * m[None, :] % (2 * total))
    angle = 2 * math.pi / lanes * (m[:, None] * m[None, :] % lanes)
    cos, sin = np.cos(angle), np.sin(angle)
    second = np.block([[cos, -sin], [sin, cos]])
    a_high, a_low = halves(first)
    b_high, b_low = halves(first.T)
    g_high, g_low = halves(second)
    return dict(
        into=np.concatenate([a_high, a_low], axis=1)[:, order + [blocks + n for n in order]],
        into3=np.concatenate([a_high, a_high, a_low], axis=1),
        out=np.block([[b_high, b_high], [b_low, np.zeros_like(b_low)]]),
        turn_cos=np.cos(turn).astype(np.float32),
        turn_sin=np.sin(turn).astype(np.float32),
        g_high=g_high,
        g_low=g_low,
    )


def dot(a, b):
    return jnp.dot(a, b, preferred_element_type=F32)


def split(x):
    high = x.astype(BF)
    return high, (x - high.astype(F32)).astype(BF)


def across(z_high, z_low, g_high, g_low):
    return dot(z_high, g_high) + dot(z_low, g_high) + dot(z_high, g_low)


def turned(part, blocks, cos, sin):
    re, im = part[:blocks], part[blocks:]
    return jnp.concatenate([re * cos + im * sin, im * cos - re * sin], axis=1)


def back_to_positions(spec, out_ref, cos, sin, blocks, lanes):
    count = spec.shape[0] // blocks
    result = []
    for pair in range(count // 2):
        rows = []
        for one in range(2):
            c = 2 * pair + one
            block = spec[c * blocks:(c + 1) * blocks]
            im, re = block[:, :lanes], block[:, lanes:]
            rows.append(jnp.concatenate([re * cos - im * sin, im * cos + re * sin], axis=0))
        both = jnp.concatenate(rows, axis=1)
        high, low = split(both)
        y = dot(out_ref[...], jnp.concatenate([high, low], axis=0))
        y = y[:blocks] + y[blocks:]
        result += [y[:, :lanes], y[:, lanes:]]
    return result


def filter_kernel(scale, f_ref, into3_ref, cos_ref, sin_ref, gh_ref, gl_ref, spec_ref):
    share, blocks, lanes = f_ref.shape
    cos, sin = cos_ref[...], sin_ref[...]
    rows = []
    for pair in range(share // 2):
        x = jnp.concatenate([f_ref[2 * pair], f_ref[2 * pair + 1]], axis=1)
        high, low = split(x)
        part = dot(into3_ref[...], jnp.concatenate([high, low, high], axis=0))
        rows.append(turned(part[:, :lanes], blocks, cos, sin))
        rows.append(turned(part[:, lanes:], blocks, cos, sin))
    high, low = split(jnp.concatenate(rows, axis=0))
    spec_ref[...] = across(high, low, gh_ref[...], gl_ref[...]) * scale


def conv_kernel(
    scale, x_ref, filt_ref, into_ref, out_tab_ref, cos_ref, sin_ref, gh_ref, gl_ref,
    y_ref, taps_ref, wide_ref, wide_taps_ref, high_ref, low_ref, spec_ref, inner_ref,
):
    blocks, fields, lanes = x_ref.shape
    share = fields // 2
    step = 2 * blocks
    half = share // 2
    cos, sin = cos_ref[...], sin_ref[...]
    wide_ref[...] = x_ref[...].astype(F32).reshape(blocks * fields, lanes)

    def put(i, parts):
        high, low = split(jnp.concatenate(parts, axis=1))
        high_ref[i * step:(i + 1) * step] = high
        low_ref[i * step:(i + 1) * step] = low

    def transform(count, out_ref):
        for start in range(0, count * step, CHUNK):
            rows = slice(start, min(start + CHUNK, count * step))
            out_ref[rows] = across(high_ref[rows], low_ref[rows], gh_ref[...], gl_ref[...])

    for i in range(share):
        x = jnp.concatenate(
            [wide_ref[pl.ds(2 * i + one, blocks, stride=fields), :] for one in range(2)], axis=1
        ).astype(BF)
        part = dot(into_ref[...], jnp.concatenate([x, x], axis=0))
        turns = [turned(part[:, one * lanes:(one + 1) * lanes], blocks, cos, sin) for one in range(2)]
        put(i, [jnp.concatenate(turns, axis=0)])
    transform(share, spec_ref)
    for i in range(half):
        xs = spec_ref[i * step:(i + 1) * step]
        gs = spec_ref[(half + i) * step:(half + i + 1) * step]
        fs = filt_ref[i * step:(i + 1) * step]
        xr, xi, gr, gi = xs[:, :lanes], xs[:, lanes:], gs[:, :lanes], gs[:, lanes:]
        fr, fi = fs[:, :lanes], fs[:, lanes:]
        put(i, [fr * xi + fi * xr, fr * xr - fi * xi])
        put(half + i, [fr * gi - fi * gr, fr * gr + fi * gi])
        put(share + i, [scale * (xr * gi - xi * gr), scale * (xr * gr + xi * gi)])
    transform(share + half, inner_ref)
    for i in range(share + half):
        inner = inner_ref[i * step:(i + 1) * step]
        for one, y in enumerate(back_to_positions(inner, out_tab_ref, cos, sin, blocks, lanes)):
            field = 2 * i + one
            if field < fields:
                wide_ref[pl.ds(field, blocks, stride=fields), :] = y
            else:
                wide_taps_ref[pl.ds(field - fields, blocks, stride=share), :] = y
    y_ref[...] = wide_ref[...].reshape(blocks, fields, lanes).astype(BF)
    taps_ref[...] = wide_taps_ref[...].astype(BF)


def mix_kernel(q_hbm, k_hbm, v_hbm, g_hbm, out_ref, q_ref, k_ref, v_ref, g_ref, sems):
    groups, fields, lanes = out_ref.shape
    share = fields // 2
    copies = [
        pltpu.make_async_copy(source, target, sems.at[i])
        for i, (source, target) in enumerate(
            [(k_hbm, k_ref), (v_hbm, v_ref), (g_hbm, g_ref), (q_hbm, q_ref)]
        )
    ]
    for copy in copies:
        copy.start()

    def turn(a, b):
        prod = (a[0].astype(F32) * b[0].astype(F32)).astype(BF).astype(F32)
        return prod.T.reshape(groups, share, lanes)

    copies[0].wait()
    copies[1].wait()
    mixed = turn(k_ref, v_ref)
    copies[2].wait()
    copies[3].wait()
    both = jnp.concatenate([mixed, turn(g_ref, q_ref)], axis=1).astype(BF)
    for place, group in enumerate(spread(groups)[::PLANE]):
        out_ref[place * PLANE:(place + 1) * PLANE] = both[group:group + PLANE]


def gate_kernel(y_ref, mine_ref, other_ref, q_ref, k_ref, v_ref, g_ref, go_ref, gq_ref, gk_ref, gv_ref, taps_ref):
    taps_ref[...] = mine_ref[...].astype(F32) + other_ref[...].astype(F32)
    groups, fields, lanes = y_ref.shape
    share = fields // 2
    both = y_ref[...].astype(F32)
    conv = both[:, :share].reshape(groups * share, lanes).T
    back = both[:, share:].reshape(groups * share, lanes).T
    go_ref[0] = (q_ref[0].astype(F32) * conv).astype(BF)
    gq_ref[0] = (g_ref[0].astype(F32) * conv).astype(BF)
    gk_ref[0] = (back * v_ref[0].astype(F32)).astype(BF)
    gv_ref[0] = (back * k_ref[0].astype(F32)).astype(BF)


PARAMS = pltpu.CompilerParams(vmem_limit_bytes=32 * 1024 * 1024)


def on_device(query_proj, key_proj, value_proj, long_filter, grad_output):
    tok_count = query_proj.shape[1]
    width = query_proj.shape[2]
    groups = lax.axis_size("ctx")
    seqs = lax.axis_size("dp")
    seq_len = tok_count * groups
    share = width // groups
    t = make_tables(groups, tok_count)
    spec_rows = share * groups

    both = pl.pallas_call(
        mix_kernel,
        out_shape=jax.ShapeDtypeStruct((groups, 2 * share, tok_count), BF),
        in_specs=[pl.BlockSpec(memory_space=pltpu.HBM)] * 4,
        scratch_shapes=[pltpu.VMEM(query_proj.shape, BF)] * 4 + [pltpu.SemaphoreType.DMA((4,))],
        compiler_params=pltpu.CompilerParams(vmem_limit_bytes=60 * 1024 * 1024),
    )(query_proj, key_proj, value_proj, grad_output)
    both = lax.all_to_all(both, "ctx", 0, 0, axis_index_groups=[spread(groups)])

    filt_spec = pl.pallas_call(
        lambda *refs: filter_kernel(2.0 / (2 * seq_len), *refs),
        out_shape=jax.ShapeDtypeStruct((spec_rows, 2 * tok_count), F32),
        compiler_params=PARAMS,
    )(long_filter.T.reshape(share, groups, tok_count), t["into3"], t["turn_cos"], t["turn_sin"], t["g_high"], t["g_low"])

    factor = 1.0 / math.sqrt(seq_len * seqs)
    out, taps = pl.pallas_call(
        lambda *refs: conv_kernel(factor * 2.0 / (2 * seq_len), *refs),
        out_shape=(
            jax.ShapeDtypeStruct((groups, 2 * share, tok_count), BF),
            jax.ShapeDtypeStruct((spec_rows, tok_count), BF),
        ),
        scratch_shapes=[
            pltpu.VMEM((2 * spec_rows, tok_count), F32),
            pltpu.VMEM((spec_rows, tok_count), F32),
            pltpu.VMEM((3 * spec_rows, 2 * tok_count), BF),
            pltpu.VMEM((3 * spec_rows, 2 * tok_count), BF),
            pltpu.VMEM((2 * spec_rows, 2 * tok_count), F32),
            pltpu.VMEM((3 * spec_rows, 2 * tok_count), F32),
        ],
        compiler_params=PARAMS,
    )(both, filt_spec, t["into"], t["out"], t["turn_cos"], t["turn_sin"], t["g_high"], t["g_low"])
    out = lax.all_to_all(out, "ctx", 0, 0)

    def swap(part, flips):
        pairs = [
            (d * groups + c, (d ^ flips[c % 2]) * groups + c) for d in range(seqs) for c in range(groups)
        ]
        return lax.ppermute(part, ("dp", "ctx"), pairs)

    def add(a, b):
        return (a.astype(F32) + b.astype(F32)).astype(BF)

    taps = add(taps, swap(taps, (2, 6)))
    taps = add(taps, swap(taps, (6, 1)))
    other = swap(taps, (1, 2))

    *grads, grad_filter = pl.pallas_call(
        gate_kernel,
        out_shape=[jax.ShapeDtypeStruct(query_proj.shape, BF)] * 4 + [jax.ShapeDtypeStruct(taps.shape, F32)],
        compiler_params=PARAMS,
    )(out, taps, other, query_proj, key_proj, value_proj, grad_output)
    grad_filter = grad_filter.reshape(groups, share, tok_count).transpose(0, 2, 1).reshape(seq_len, share)
    return (*grads, grad_filter)


def solution(mesh):
    tokens = P("dp", "ctx", None)
    taps = P(None, "ctx")
    return jax.shard_map(
        on_device,
        mesh=mesh,
        in_specs=(tokens, tokens, tokens, taps, tokens),
        out_specs=(tokens, tokens, tokens, tokens, taps),
        check_vma=False,
    )
```

```python
import math

import jax
import jax.numpy as jnp
import ml_dtypes
import numpy as np
from jax import lax
from jax.experimental import pallas as pl
from jax.experimental.pallas import tpu as pltpu
from jax.sharding import PartitionSpec as P

BF = jnp.bfloat16
F32 = jnp.float32
CHUNK = 256
PLANE = 4


def halves(table):
    high = table.astype(np.float32).astype(ml_dtypes.bfloat16)
    low = (table - high.astype(np.float64)).astype(np.float32).astype(ml_dtypes.bfloat16)
    return high, low


def spread(groups):
    planes = groups // PLANE
    bits = planes.bit_length() - 1
    reverse = [int(format(z, f"0{bits}b")[::-1], 2) for z in range(planes)]
    return [z * PLANE + one for z in reverse for one in range(PLANE)]


def make_tables(blocks, lanes):
    order = spread(blocks)
    period = 2 * blocks
    total = period * lanes
    n = np.arange(blocks)
    odd = 2 * np.arange(blocks) + 1
    angle = math.pi / period * (n[None, :] * odd[:, None] % (2 * period))
    first = np.concatenate([np.cos(angle), -np.sin(angle)])
    m = np.arange(lanes)
    turn = math.pi / total * (odd[:, None] * m[None, :] % (2 * total))
    angle = 2 * math.pi / lanes * (m[:, None] * m[None, :] % lanes)
    cos, sin = np.cos(angle), np.sin(angle)
    second = np.block([[cos, -sin], [sin, cos]])
    a_high, a_low = halves(first)
    b_high, b_low = halves(first.T)
    g_high, g_low = halves(second)
    return dict(
        into=np.concatenate([a_high, a_low], axis=1)[:, order + [blocks + n for n in order]],
        into3=np.concatenate([a_high, a_high, a_low], axis=1),
        out=np.block([[b_high, b_high], [b_low, np.zeros_like(b_low)]]),
        turn_cos=np.cos(turn).astype(np.float32),
        turn_sin=np.sin(turn).astype(np.float32),
        g_high=g_high,
        g_low=g_low,
    )


def dot(a, b):
    return jnp.dot(a, b, preferred_element_type=F32)


def split(x):
    high = x.astype(BF)
    return high, (x - high.astype(F32)).astype(BF)


def across(z_high, z_low, g_high, g_low):
    return dot(z_high, g_high) + dot(z_low, g_high) + dot(z_high, g_low)


def turned(part, blocks, cos, sin):
    re, im = part[:blocks], part[blocks:]
    return jnp.concatenate([re * cos + im * sin, im * cos - re * sin], axis=1)


def back_to_positions(spec, out_ref, cos, sin, blocks, lanes):
    count = spec.shape[0] // blocks
    result = []
    for pair in range(count // 2):
        rows = []
        for one in range(2):
            c = 2 * pair + one
            block = spec[c * blocks:(c + 1) * blocks]
            im, re = block[:, :lanes], block[:, lanes:]
            rows.append(jnp.concatenate([re * cos - im * sin, im * cos + re * sin], axis=0))
        both = jnp.concatenate(rows, axis=1)
        high, low = split(both)
        y = dot(out_ref[...], jnp.concatenate([high, low], axis=0))
        y = y[:blocks] + y[blocks:]
        result += [y[:, :lanes], y[:, lanes:]]
    return result


def filter_kernel(scale, f_ref, into3_ref, cos_ref, sin_ref, gh_ref, gl_ref, spec_ref):
    share, blocks, lanes = f_ref.shape
    cos, sin = cos_ref[...], sin_ref[...]
    rows = []
    for pair in range(share // 2):
        x = jnp.concatenate([f_ref[2 * pair], f_ref[2 * pair + 1]], axis=1)
        high, low = split(x)
        part = dot(into3_ref[...], jnp.concatenate([high, low, high], axis=0))
        rows.append(turned(part[:, :lanes], blocks, cos, sin))
        rows.append(turned(part[:, lanes:], blocks, cos, sin))
    high, low = split(jnp.concatenate(rows, axis=0))
    spec_ref[...] = across(high, low, gh_ref[...], gl_ref[...]) * scale


def conv_kernel(
    scale, x_ref, filt_ref, into_ref, out_tab_ref, cos_ref, sin_ref, gh_ref, gl_ref,
    y_ref, taps_ref, wide_ref, wide_taps_ref, high_ref, low_ref, spec_ref, inner_ref,
):
    blocks, fields, lanes = x_ref.shape
    share = fields // 2
    step = 2 * blocks
    half = share // 2
    cos, sin = cos_ref[...], sin_ref[...]
    wide_ref[...] = x_ref[...].astype(F32).reshape(blocks * fields, lanes)

    def put(i, parts):
        high, low = split(jnp.concatenate(parts, axis=1))
        high_ref[i * step:(i + 1) * step] = high
        low_ref[i * step:(i + 1) * step] = low

    def transform(count, out_ref):
        for start in range(0, count * step, CHUNK):
            rows = slice(start, min(start + CHUNK, count * step))
            out_ref[rows] = across(high_ref[rows], low_ref[rows], gh_ref[...], gl_ref[...])

    for i in range(share):
        x = jnp.concatenate(
            [wide_ref[pl.ds(2 * i + one, blocks, stride=fields), :] for one in range(2)], axis=1
        ).astype(BF)
        part = dot(into_ref[...], jnp.concatenate([x, x], axis=0))
        turns = [turned(part[:, one * lanes:(one + 1) * lanes], blocks, cos, sin) for one in range(2)]
        put(i, [jnp.concatenate(turns, axis=0)])
    transform(share, spec_ref)
    for i in range(half):
        xs = spec_ref[i * step:(i + 1) * step]
        gs = spec_ref[(half + i) * step:(half + i + 1) * step]
        fs = filt_ref[i * step:(i + 1) * step]
        xr, xi, gr, gi = xs[:, :lanes], xs[:, lanes:], gs[:, :lanes], gs[:, lanes:]
        fr, fi = fs[:, :lanes], fs[:, lanes:]
        put(i, [fr * xi + fi * xr, fr * xr - fi * xi])
        put(half + i, [fr * gi - fi * gr, fr * gr + fi * gi])
        put(share + i, [scale * (xr * gi - xi * gr), scale * (xr * gr + xi * gi)])
    transform(share + half, inner_ref)
    for i in range(share + half):
        inner = inner_ref[i * step:(i + 1) * step]
        for one, y in enumerate(back_to_positions(inner, out_tab_ref, cos, sin, blocks, lanes)):
            field = 2 * i + one
            if field < fields:
                wide_ref[pl.ds(field, blocks, stride=fields), :] = y
            else:
                wide_taps_ref[pl.ds(field - fields, blocks, stride=share), :] = y
    ys = wide_ref[...].reshape(blocks, fields, lanes).astype(BF)
    for place, block in enumerate(spread(blocks)[::PLANE]):
        y_ref[place * PLANE:(place + 1) * PLANE] = ys[block:block + PLANE]
    taps_ref[...] = wide_taps_ref[...].astype(BF)


def mix_kernel(q_hbm, k_hbm, v_hbm, g_hbm, out_ref, q_ref, k_ref, v_ref, g_ref, sems):
    groups, fields, lanes = out_ref.shape
    share = fields // 2
    copies = [
        pltpu.make_async_copy(source, target, sems.at[i])
        for i, (source, target) in enumerate(
            [(k_hbm, k_ref), (v_hbm, v_ref), (g_hbm, g_ref), (q_hbm, q_ref)]
        )
    ]
    for copy in copies:
        copy.start()

    def turn(a, b):
        prod = (a[0].astype(F32) * b[0].astype(F32)).astype(BF).astype(F32)
        return prod.T.reshape(groups, share, lanes)

    copies[0].wait()
    copies[1].wait()
    mixed = turn(k_ref, v_ref)
    copies[2].wait()
    copies[3].wait()
    both = jnp.concatenate([mixed, turn(g_ref, q_ref)], axis=1).astype(BF)
    for place, group in enumerate(spread(groups)[::PLANE]):
        out_ref[place * PLANE:(place + 1) * PLANE] = both[group:group + PLANE]


def gate_kernel(y_ref, mine_ref, other_ref, q_ref, k_ref, v_ref, g_ref, go_ref, gq_ref, gk_ref, gv_ref, taps_ref):
    taps_ref[...] = mine_ref[...].astype(F32) + other_ref[...].astype(F32)
    groups, fields, lanes = y_ref.shape
    share = fields // 2
    places = np.argsort(spread(groups)[::PLANE]) * PLANE
    both = jnp.concatenate([y_ref[int(place):int(place) + PLANE] for place in places], axis=0).astype(F32)
    conv = both[:, :share].reshape(groups * share, lanes).T
    back = both[:, share:].reshape(groups * share, lanes).T
    go_ref[0] = (q_ref[0].astype(F32) * conv).astype(BF)
    gq_ref[0] = (g_ref[0].astype(F32) * conv).astype(BF)
    gk_ref[0] = (back * v_ref[0].astype(F32)).astype(BF)
    gv_ref[0] = (back * k_ref[0].astype(F32)).astype(BF)


PARAMS = pltpu.CompilerParams(vmem_limit_bytes=32 * 1024 * 1024)


def on_device(query_proj, key_proj, value_proj, long_filter, grad_output):
    tok_count = query_proj.shape[1]
    width = query_proj.shape[2]
    groups = lax.axis_size("ctx")
    seqs = lax.axis_size("dp")
    seq_len = tok_count * groups
    share = width // groups
    t = make_tables(groups, tok_count)
    spec_rows = share * groups

    both = pl.pallas_call(
        mix_kernel,
        out_shape=jax.ShapeDtypeStruct((groups, 2 * share, tok_count), BF),
        in_specs=[pl.BlockSpec(memory_space=pltpu.HBM)] * 4,
        scratch_shapes=[pltpu.VMEM(query_proj.shape, BF)] * 4 + [pltpu.SemaphoreType.DMA((4,))],
        compiler_params=pltpu.CompilerParams(vmem_limit_bytes=60 * 1024 * 1024),
    )(query_proj, key_proj, value_proj, grad_output)
    both = lax.all_to_all(both, "ctx", 0, 0, axis_index_groups=[spread(groups)])

    filt_spec = pl.pallas_call(
        lambda *refs: filter_kernel(2.0 / (2 * seq_len), *refs),
        out_shape=jax.ShapeDtypeStruct((spec_rows, 2 * tok_count), F32),
        compiler_params=PARAMS,
    )(long_filter.T.reshape(share, groups, tok_count), t["into3"], t["turn_cos"], t["turn_sin"], t["g_high"], t["g_low"])

    factor = 1.0 / math.sqrt(seq_len * seqs)
    out, taps = pl.pallas_call(
        lambda *refs: conv_kernel(factor * 2.0 / (2 * seq_len), *refs),
        out_shape=(
            jax.ShapeDtypeStruct((groups, 2 * share, tok_count), BF),
            jax.ShapeDtypeStruct((spec_rows, tok_count), BF),
        ),
        scratch_shapes=[
            pltpu.VMEM((2 * spec_rows, tok_count), F32),
            pltpu.VMEM((spec_rows, tok_count), F32),
            pltpu.VMEM((3 * spec_rows, 2 * tok_count), BF),
            pltpu.VMEM((3 * spec_rows, 2 * tok_count), BF),
            pltpu.VMEM((2 * spec_rows, 2 * tok_count), F32),
            pltpu.VMEM((3 * spec_rows, 2 * tok_count), F32),
        ],
        compiler_params=PARAMS,
    )(both, filt_spec, t["into"], t["out"], t["turn_cos"], t["turn_sin"], t["g_high"], t["g_low"])
    out = lax.all_to_all(out, "ctx", 0, 0, axis_index_groups=[spread(groups)])

    def swap(part, flips):
        pairs = [
            (d * groups + c, (d ^ flips[c % 2]) * groups + c) for d in range(seqs) for c in range(groups)
        ]
        return lax.ppermute(part, ("dp", "ctx"), pairs)

    def add(a, b):
        return (a.astype(F32) + b.astype(F32)).astype(BF)

    taps = add(taps, swap(taps, (2, 6)))
    taps = add(taps, swap(taps, (6, 1)))
    other = swap(taps, (1, 2))

    *grads, grad_filter = pl.pallas_call(
        gate_kernel,
        out_shape=[jax.ShapeDtypeStruct(query_proj.shape, BF)] * 4 + [jax.ShapeDtypeStruct(taps.shape, F32)],
        compiler_params=PARAMS,
    )(out, taps, other, query_proj, key_proj, value_proj, grad_output)
    grad_filter = grad_filter.reshape(groups, share, tok_count).transpose(0, 2, 1).reshape(seq_len, share)
    return (*grads, grad_filter)


def solution(mesh):
    tokens = P("dp", "ctx", None)
    taps = P(None, "ctx")
    return jax.shard_map(
        on_device,
        mesh=mesh,
        in_specs=(tokens, tokens, tokens, taps, tokens),
        out_specs=(tokens, tokens, tokens, tokens, taps),
        check_vma=False,
    )
```
